256 devices in a mesh: frame: 32 (over y_hi, z, core), head: 8 (over x, y_lo).
Axes of the slice: x: 4, y: 4 (y_hi: 2, y_lo: 2; y = y_hi * 2 + y_lo), z: 8, core: 2. Of those that a mesh axis runs over, the one named last changes fastest.
Arguments:
- tokens: bfloat16 [16384, 3072], P(('frame', 'head')), may hold values from -6 to 6
- norm_gain: float32 [3072], replicated, may hold values from 0.25 to 1.75
- w_query: bfloat16 [3072, 2048], P(None, 'head'), may hold values from -0.109375 to 0.109375
- w_key: bfloat16 [3072, 2048], P(None, 'head'), may hold values from -0.109375 to 0.109375
- w_value: bfloat16 [3072, 2048], P(None, 'head'), may hold values from -0.109375 to 0.109375
- query_gain: float32 [128], replicated, may hold values from 0.8 to 2
- key_gain: float32 [128], replicated, may hold values from 0.8 to 2
- w_out: bfloat16 [2048, 3072], P('head'), may hold values from -0.5 to 0.5
- block_lists: int32 [128, 6], P('frame'), may hold values from -1 to 127, as said below
- block_counts: int32 [128], P('frame'), may hold values from 1 to 6, as said below
Outputs:
- attended: bfloat16 [16384, 3072], P(('frame', 'head'))
The draws below stay inside these ranges and needn't reach their ends.
Inputs may be any that keep to these rules, and one draw needn't show every extreme that they name: `block_lists`: row i holds block_counts[i] distinct key block numbers, then -1 in the remaining slots; its first entry is i itself; every listed j satisfies |j // 4 - i // 4| <= 2. `block_counts`: some row has 6 live entries.
All inputs are finite; a program needn't handle non-finite values.
Results may differ from the reference program's by a relative error of at most 0.019.
Values may be sent and summed in bfloat16 or wider, within the bound.
A program may use at most 64 MiB of HBM per device.

```python
import math
import jax
import jax.numpy as jnp
from jax import lax

D = 3072
H = 16
HD = 128
BLK = 128
MAXB = 6
BAND = 2
NB = 4
NKB = 128
TOKENS = 16384
N_HEAD = 8


def band_mask(key):
    slot_count = (2 * BAND + 1) * NB
    frames = NKB // NB
    query_block = jnp.arange(NKB, dtype=jnp.int32)
    column = jnp.arange(slot_count, dtype=jnp.int32)
    device = query_block[:, None] // NB - BAND + column[None, :] // NB
    block_number = device * NB + column[None, :] % NB
    inside = (device >= 0) & (device < frames)
    own_slot = column[None, :] == BAND * NB + query_block[:, None] % NB
    raw_scores = jax.random.randint(jax.random.fold_in(key, 11), (NKB, slot_count), 0, 1 << 20)
    ranking = jnp.where(own_slot, 1 << 30, jnp.where(inside, raw_scores * slot_count + column[None, :], -1 - column[None, :]))
    top_values, top_index = lax.top_k(ranking, MAXB)
    chosen = jnp.take_along_axis(block_number, top_index, axis=1)
    counts = jax.random.randint(jax.random.fold_in(key, 12), (NKB,), 1, MAXB + 1)
    counts = counts.at[0].set(MAXB)
    listed = jnp.arange(MAXB, dtype=jnp.int32)[None, :] < counts[:, None]
    return (jnp.where(listed, chosen, -1).astype(jnp.int32), counts.astype(jnp.int32))


def draw_block_lists(key, part):
    shared = band_mask(key)
    return shared[0]


def draw_block_counts(key, part):
    shared = band_mask(key)
    return shared[1]


def block_levels(stream_key, shape, pieces, least, high):
    def one(axis_at, blocks):
        draws = jax.random.uniform(jax.random.fold_in(jax.random.fold_in(stream_key, 6), axis_at), (blocks,), jnp.float32, least / len(pieces), high / len(pieces))
        return jnp.repeat(jnp.exp(draws), shape[axis_at] // blocks).reshape((-1,) + (1,) * (len(shape) - axis_at - 1))

    level = one(*pieces[0])
    for cut in pieces[1:]:
        level = level * one(*cut)
    return level


def bell_draw(stream_key, dims, scale, bound, cuts=(), kind=jnp.bfloat16):
    result = jax.random.normal(stream_key, dims, jnp.float32) * scale
    if len(cuts) > 0:
        result = block_levels(stream_key, dims, cuts, -0.22, 0.18) * result
    return jnp.clip(result, min=-bound, max=bound).astype(kind)


def setup_inputs(seed: int = 0) -> dict:
    arg_keys = jax.random.split(jax.random.key(seed), 11)
    return {
        "tokens": bell_draw(arg_keys[0], (TOKENS, D), 1.0, 6.0, ((0, 256),)),
        "norm_gain": jnp.clip(1.0 + 0.15 * jax.random.normal(arg_keys[1], (D,), jnp.float32), 0.25, 1.75),
        "w_query": bell_draw(arg_keys[2], (D, H * HD), D ** -0.5, 0.109375, ((1, 8),)),
        "w_key": bell_draw(arg_keys[3], (D, H * HD), D ** -0.5, 0.109375, ((1, 8),)),
        "w_value": bell_draw(arg_keys[4], (D, H * HD), D ** -0.5, 0.109375, ((1, 8),)),
        "query_gain": jnp.clip(jnp.exp(jax.random.uniform(arg_keys[5], (HD,), jnp.float32, math.log(0.8), math.log(2.0))), 0.8, 2.0),
        "key_gain": jnp.clip(jnp.exp(jax.random.uniform(arg_keys[6], (HD,), jnp.float32, math.log(0.8), math.log(2.0))), 0.8, 2.0),
        "w_out": bell_draw(arg_keys[7], (H * HD, D), HD ** -0.5, 0.5, ((0, 8),)),
        "block_lists": draw_block_lists(jax.random.fold_in(arg_keys[10], 71), 0),
        "block_counts": draw_block_counts(jax.random.fold_in(arg_keys[10], 71), 0),
    }


def norm_heads(normed, weight, gain):
    projected = jnp.dot(normed, weight, preferred_element_type=jnp.float32).reshape(TOKENS, H, HD)
    factor = lax.rsqrt(lax.optimization_barrier(jnp.mean(projected * projected, axis=-1, keepdims=True)) + 1e-06)
    return (projected * factor * gain).astype(jnp.bfloat16)

def reference(tokens, norm_gain, w_query, w_key, w_value, query_gain, key_gain, w_out, block_lists, block_counts):
    wide = tokens.astype(jnp.float32)
    normed = (wide * lax.rsqrt(lax.optimization_barrier(jnp.mean(wide * wide, axis=-1, keepdims=True)) + 1e-06) * norm_gain).astype(jnp.bfloat16)
    queries = norm_heads(normed, w_query, query_gain)
    keys = norm_heads(normed, w_key, key_gain)
    values = jnp.dot(normed, w_value, preferred_element_type=jnp.float32).astype(jnp.bfloat16).reshape(TOKENS, H, HD)
    key_blocks = keys.reshape(NKB, BLK, H, HD)
    value_blocks = values.reshape(NKB, BLK, H, HD)
    factor = 1.0 / HD ** 0.5

    def one_block(index):
        query_rows = lax.dynamic_slice_in_dim(queries, (index * BLK).astype(jnp.int32), BLK, 0)
        picks = block_lists[index]
        listed = jnp.arange(MAXB, dtype=jnp.int32) < block_counts[index]
        safe_picks = jnp.where(listed, picks, 0).astype(jnp.int32)
        keys_here = key_blocks[safe_picks].reshape(MAXB * BLK, H, HD)
        values_here = value_blocks[safe_picks].reshape(MAXB * BLK, H, HD)
        scores = jnp.einsum('qhd,khd->hqk', query_rows.astype(jnp.float32), keys_here.astype(jnp.float32)) * factor
        allowed = jnp.repeat(listed, BLK)
        weights = jnp.where(allowed[None, None, :], jnp.exp(scores), 0.0)
        totals = lax.optimization_barrier(jnp.sum(weights, axis=-1))
        rounded = weights.astype(jnp.bfloat16)
        weighted = jnp.einsum('hqk,khd->qhd', rounded.astype(jnp.float32), values_here.astype(jnp.float32))
        return (weighted / jnp.transpose(totals)[:, :, None]).astype(jnp.bfloat16)
    context = lax.map(one_block, jnp.arange(NKB, dtype=jnp.int32)).reshape(TOKENS, H * HD)
    group_width = H * HD // N_HEAD
    summed = jnp.zeros((TOKENS, D), jnp.float32)
    for group in range(N_HEAD):
        partial_sum = jnp.dot(context[:, group * group_width:(group + 1) * group_width], w_out[group * group_width:(group + 1) * group_width, :], preferred_element_type=jnp.float32)
        summed = summed + partial_sum.astype(jnp.bfloat16).astype(jnp.float32)
    return summed.astype(jnp.bfloat16)
```

```python
import functools

import jax
import jax.numpy as jnp
from jax import lax
from jax.experimental import pallas as pl
from jax.experimental.pallas import tpu as pltpu
from jax.sharding import PartitionSpec as P

HD = 128
BLK = 128
MAXB = 6
BAND = 2
EPS = 1e-06
MESH = pl.DeviceIdType.MESH


def kernel(
    frames,
    tokens_ref,
    ngain_ref,
    qgain_ref,
    kgain_ref,
    lists_ref,
    counts_ref,
    wq_hbm,
    wk_hbm,
    wv_hbm,
    wo_hbm,
    out_ref,
    wq,
    wk,
    wv,
    wo,
    xn,
    q,
    kv,
    part,
    got_a,
    got_h,
    got_b,
    got_c,
    got_d,
    w_sem,
    ag_s,
    ag_r,
    kv_s,
    kv_r,
    rs_s,
    rs_r,
):
    f = lax.axis_index("frame")
    head = lax.axis_index("head")
    x, y = head // 2, head % 2
    other = 1 - y
    right, left, opposite = (x + 1) % 4, (x + 3) % 4, (x + 2) % 4
    dev_right, dev_left, dev_other = right * 2 + y, left * 2 + y, x * 2 + other
    rows = tokens_ref.shape[0]
    half = rows // 2
    width = wq.shape[1]
    heads = width // HD
    reach = [d for d in range(-BAND, BAND + 1) if d != 0]

    weights = [
        pltpu.make_async_copy(src, dst, w_sem.at[i])
        for i, (src, dst) in enumerate(((wq_hbm, wq), (wk_hbm, wk), (wv_hbm, wv), (wo_hbm, wo)))
    ]
    for copy in weights:
        copy.start()

    def within(d):
        return jnp.logical_and(f + d >= 0, f + d < frames)

    barrier = pltpu.get_barrier_semaphore()
    for device in (dev_right, dev_left, dev_other):
        pl.semaphore_signal(barrier, inc=1, device_id={"head": device}, device_id_type=MESH)
    for d in reach:

        @pl.when(within(d))
        def _():
            pl.semaphore_signal(barrier, inc=1, device_id={"frame": f + d}, device_id_type=MESH)

    wide = tokens_ref[...].astype(jnp.float32)
    factor = lax.rsqrt(jnp.mean(wide * wide, axis=-1, keepdims=True) + EPS)
    xn[0] = (wide * factor * ngain_ref[...]).astype(jnp.bfloat16)

    peers = 3
    for d in reach:
        peers = peers + jnp.where(within(d), 1, 0)
    pl.semaphore_wait(barrier, peers)

    def send(src, dst, sems, index, device):
        return pltpu.make_async_remote_copy(
            src_ref=src,
            dst_ref=dst,
            send_sem=sems[0].at[index],
            recv_sem=sems[1].at[index],
            device_id={"head": device},
            device_id_type=MESH,
        )

    ag = (ag_s, ag_r)
    low, high = pl.ds(0, half), pl.ds(half, half)
    a_right = send(xn.at[0], xn.at[2], ag, 0, dev_right)
    a_left = send(xn.at[0], xn.at[3], ag, 1, dev_left)
    b_other = send(xn.at[0], xn.at[1], ag, 2, dev_other)
    f_right = send(xn.at[2, high], xn.at[4, high], ag, 3, dev_right)
    f_left = send(xn.at[3, low], xn.at[4, low], ag, 4, dev_left)
    c_right = send(xn.at[1], xn.at[5], ag, 5, dev_right)
    c_left = send(xn.at[1], xn.at[6], ag, 6, dev_left)
    d_high = send(xn.at[4, high], xn.at[7, high], ag, 7, dev_other)
    d_low = send(xn.at[4, low], xn.at[7, low], ag, 8, dev_other)

    slot_head = [
        head,
        dev_other,
        dev_left,
        dev_right,
        opposite * 2 + y,
        left * 2 + other,
        right * 2 + other,
        opposite * 2 + other,
    ]

    def normed_heads(section, gain_ref):
        done = []
        for i in range(heads):
            part_i = section[:, i * HD : (i + 1) * HD]
            scale = lax.rsqrt(jnp.mean(part_i * part_i, axis=-1, keepdims=True) + EPS)
            done.append((part_i * scale * gain_ref[...]).astype(jnp.bfloat16))
        return done

    def project(slot):
        at = slot_head[slot]
        mine = BAND * 8 + at
        block = xn[slot]
        keys = jnp.dot(block, wk[...], preferred_element_type=jnp.float32)
        for i, piece in enumerate(normed_heads(keys, kgain_ref)):
            kv[mine, :, i * HD : (i + 1) * HD] = piece
        values = jnp.dot(block, wv[...], preferred_element_type=jnp.float32)
        kv[mine, :, width:] = values.astype(jnp.bfloat16)
        for i, d in enumerate(reach):

            @pl.when(within(d))
            def _():
                pltpu.make_async_remote_copy(
                    src_ref=kv.at[mine],
                    dst_ref=kv.at[(BAND - d) * 8 + at],
                    send_sem=kv_s.at[i],
                    recv_sem=kv_r.at[i],
                    device_id={"frame": f + d},
                    device_id_type=MESH,
                ).start()

        queries = jnp.dot(block, wq[...], preferred_element_type=jnp.float32)
        for i, piece in enumerate(normed_heads(queries, qgain_ref)):
            q[at, :, i * HD : (i + 1) * HD] = piece

    a_right.start()
    a_left.start()
    b_other.start()
    for copy in weights:
        copy.wait()
    project(0)
    b_other.wait_recv()
    c_right.start()
    c_left.start()
    a_right.wait_recv()
    f_right.start()
    a_left.wait_recv()
    f_left.start()
    project(1)
    project(2)
    project(3)
    f_right.wait_recv()
    d_high.start()
    f_left.wait_recv()
    d_low.start()
    project(4)
    c_right.wait_recv()
    project(5)
    c_left.wait_recv()
    project(6)
    d_high.wait_recv()
    d_low.wait_recv()
    project(7)

    def frame_copy(i, d):
        return pltpu.make_async_remote_copy(
            src_ref=kv.at[pl.ds(BAND * 8, 8)],
            dst_ref=kv.at[pl.ds((BAND - d) * 8, 8)],
            send_sem=kv_s.at[i],
            recv_sem=kv_r.at[i],
            device_id={"frame": f + d},
            device_id_type=MESH,
        )

    for i, d in enumerate(reach):

        @pl.when(within(-d))
        def _():
            frame_copy(i, d).wait_recv()

    score_factor = 1.0 / HD**0.5

    def attend(block, place):
        queries = q[pl.ds(block * 2, 2)].reshape(BLK, width)
        listed = counts_ref[block]
        weighted = [jnp.zeros((BLK, HD), jnp.float32) for _ in range(heads)]
        totals = [jnp.zeros((BLK, 1), jnp.float32) for _ in range(heads)]
        for m in range(MAXB):
            live = m < listed
            picked = jnp.where(live, lists_ref[block, m] - f * 4 + BAND * 4, BAND * 4 + block)
            picked = jnp.clip(picked, 0, 5 * 4 - 1)
            pair = kv[pl.ds(picked * 2, 2)].reshape(BLK, 2 * width)
            on = jnp.where(live, 1.0, 0.0).astype(jnp.float32)
            for i in range(heads):
                scores = lax.dot_general(
                    queries[:, i * HD : (i + 1) * HD],
                    pair[:, i * HD : (i + 1) * HD],
                    (((1,), (1,)), ((), ())),
                    preferred_element_type=jnp.float32,
                )
                weight = jnp.exp(scores * score_factor) * on
                totals[i] = totals[i] + jnp.sum(weight, axis=-1, keepdims=True)
                weighted[i] = weighted[i] + jnp.dot(
                    weight.astype(jnp.bfloat16),
                    pair[:, width + i * HD : width + (i + 1) * HD],
                    preferred_element_type=jnp.float32,
                )
        context = jnp.concatenate(
            [(weighted[i] / totals[i]).astype(jnp.bfloat16) for i in range(heads)], axis=1
        )
        partial = jnp.dot(context, wo[...], preferred_element_type=jnp.float32)
        part[place] = partial.astype(jnp.bfloat16).reshape(2, rows, partial.shape[1])

    rs = (rs_s, rs_r)
    a_send = send(part.at[0, other], got_a, rs, 0, dev_other)
    b_left = send(part.at[1, other], got_b.at[0], rs, 1, dev_left)
    b_right = send(part.at[2, other], got_b.at[1], rs, 2, dev_right)
    c_left_high = send(part.at[1, y, high], got_c.at[0, high], rs, 3, dev_left)
    c_left_low = send(part.at[1, y, low], got_c.at[0, low], rs, 4, dev_left)
    c_right_high = send(part.at[2, y, high], got_c.at[1, high], rs, 5, dev_right)
    c_right_low = send(part.at[2, y, low], got_c.at[1, low], rs, 6, dev_right)
    h_left = send(part.at[0, y, low], got_h.at[0], rs, 7, dev_left)
    h_right = send(part.at[0, y, high], got_h.at[1], rs, 8, dev_right)
    d_send = send(part.at[3, other], got_d, rs, 9, dev_other)

    def wide_sum(*terms):
        total = terms[0].astype(jnp.float32)
        for term in terms[1:]:
            total = total + term.astype(jnp.float32)
        return total.astype(jnp.bfloat16)

    attend(opposite, 0)
    a_send.start()
    attend(left, 1)
    b_left.start()
    c_left_high.start()
    attend(right, 2)
    b_right.start()
    c_right_low.start()
    attend(x, 3)

    a_send.wait_recv()
    part[0, y] = wide_sum(part[0, y], got_a[...])
    h_left.start()
    h_right.start()
    b_left.wait_recv()
    b_right.wait_recv()
    part[3, other] = wide_sum(part[3, other], got_b[0], got_b[1])
    d_send.start()
    h_left.wait_recv()
    part[1, y, 0:half] = wide_sum(part[1, y, 0:half], got_h[0])
    c_left_low.start()
    h_right.wait_recv()
    part[2, y, half:rows] = wide_sum(part[2, y, half:rows], got_h[1])
    c_right_high.start()
    for copy in (c_left_high, c_right_low, d_send, c_left_low, c_right_high):
        copy.wait_recv()
    out_ref[...] = wide_sum(part[3, y], got_c[0], got_c[1], got_d[...])

    for copy in (a_right, a_left, b_other, f_right, f_left, c_right, c_left, d_high, d_low):
        copy.wait_send()
    for i, d in enumerate(reach):

        @pl.when(within(d))
        def _():
            frame_copy(i, d).wait_send()

    for copy in (a_send, b_left, b_right, c_left_high, c_left_low, c_right_high, c_right_low):
        copy.wait_send()
    for copy in (h_left, h_right, d_send):
        copy.wait_send()


def per_device(
    tokens,
    norm_gain,
    w_query,
    w_key,
    w_value,
    query_gain,
    key_gain,
    w_out,
    block_lists,
    block_counts,
):
    rows, depth = tokens.shape
    width = w_query.shape[1]
    dma = pltpu.SemaphoreType.DMA
    bf16 = jnp.bfloat16
    vmem = pl.BlockSpec(memory_space=pltpu.VMEM)
    smem = pl.BlockSpec(memory_space=pltpu.SMEM)
    hbm = pl.BlockSpec(memory_space=pl.ANY)
    return pl.pallas_call(
        functools.partial(kernel, lax.axis_size("frame")),
        out_shape=jax.ShapeDtypeStruct((rows, depth), bf16),
        in_specs=[vmem, vmem, vmem, vmem, smem, smem, hbm, hbm, hbm, hbm],
        out_specs=vmem,
        scratch_shapes=[
            pltpu.VMEM((depth, width), bf16),
            pltpu.VMEM((depth, width), bf16),
            pltpu.VMEM((depth, width), bf16),
            pltpu.VMEM((width, depth), bf16),
            pltpu.VMEM((8, rows, depth), bf16),
            pltpu.VMEM((8, rows, width), bf16),
            pltpu.VMEM(((2 * BAND + 1) * 8, rows, 2 * width), bf16),
            pltpu.VMEM((4, 2, rows, depth), bf16),
            pltpu.VMEM((rows, depth), bf16),
            pltpu.VMEM((2, rows // 2, depth), bf16),
            pltpu.VMEM((2, rows, depth), bf16),
            pltpu.VMEM((2, rows, depth), bf16),
            pltpu.VMEM((rows, depth), bf16),
            dma((4,)),
            dma((9,)),
            dma((9,)),
            dma((2 * BAND,)),
            dma((2 * BAND,)),
            dma((10,)),
            dma((10,)),
        ],
        compiler_params=pltpu.CompilerParams(
            collective_id=0, has_side_effects=True, vmem_limit_bytes=48 * 1024 * 1024
        ),
    )(
        tokens,
        norm_gain.reshape(1, depth),
        query_gain.reshape(1, HD),
        key_gain.reshape(1, HD),
        block_lists,
        block_counts,
        w_query,
        w_key,
        w_value,
        w_out,
    )


def solution(mesh):
    placed = (
        P(("frame", "head"), None),
        P(),
        P(None, "head"),
        P(None, "head"),
        P(None, "head"),
        P(),
        P(),
        P("head", None),
        P("frame", None),
        P("frame"),
    )
    return jax.shard_map(
        per_device,
        mesh=mesh,
        in_specs=placed,
        out_specs=P(("frame", "head"), None),
        check_vma=False,
    )
```

```python
import functools

import jax
import jax.numpy as jnp
from jax import lax
from jax.experimental import pallas as pl
from jax.experimental.pallas import tpu as pltpu
from jax.sharding import PartitionSpec as P

HD = 128
BLK = 128
MAXB = 6
BAND = 2
NB = 4
EPS = 1e-06
PIECES = 4
MESH = pl.DeviceIdType.MESH

PLACE = (0, 1, 6, 2, 4, 7, 3, 5)


def kernel(
    frames,
    tokens_hbm,
    ngain_hbm,
    qgain_hbm,
    kgain_hbm,
    lists_hbm,
    counts_hbm,
    wq_hbm,
    wk_hbm,
    wv_hbm,
    wo_hbm,
    out_ref,
    tokens_ref,
    ngain_ref,
    qgain_ref,
    kgain_ref,
    lists_ref,
    counts_ref,
    wq,
    wk,
    wv,
    wo,
    xn,
    q,
    kv,
    ctx,
    part,
    got_h,
    got_c,
    in_sem,
    ag_s,
    ag_r,
    kv_s,
    kv_r,
    wo_s,
    wo_r,
    ctx_s,
    ctx_r,
    rs_s,
    rs_r,
):
    f = lax.axis_index("frame")
    head = lax.axis_index("head")
    x, y = head // 2, head % 2
    core = f % 2
    toward = 1 - 2 * core
    right, left = (x + 1) % 4, (x + 3) % 4
    to_right, to_left = {"head": right * 2 + y}, {"head": left * 2 + y}
    to_other = {"head": x * 2 + 1 - y}
    to_sibling = {"frame": f + toward}
    to_far = {"frame": f + 2 * toward}
    to_near = {"frame": f - toward}
    to_across = {"frame": (f + frames // 2) % frames, "head": x * 2 + 1 - y}
    rows = tokens_ref.shape[0]
    half, piece = rows // 2, rows // PIECES
    width = wq.shape[1]
    heads = width // HD

    def within(d):
        return jnp.logical_and(f + d >= 0, f + d < frames)

    far_to, far_from, near = within(2 * toward), within(-2 * toward), within(-toward)

    loads = [
        pltpu.make_async_copy(src, dst, in_sem.at[i])
        for i, (src, dst) in enumerate(
            (
                (tokens_hbm, tokens_ref),
                (ngain_hbm, ngain_ref),
                (qgain_hbm, qgain_ref),
                (kgain_hbm, kgain_ref),
                (lists_hbm, lists_ref),
                (counts_hbm, counts_ref),
                (wk_hbm, wk),
                (wv_hbm, wv),
                (wq_hbm, wq),
                (wo_hbm, wo.at[0:width]),
            )
        )
    ]
    for copy in loads:
        copy.start()

    barrier = pltpu.get_barrier_semaphore()

    def greet(device):
        pl.semaphore_signal(barrier, inc=1, device_id=device, device_id_type=MESH)

    for device in (to_right, to_left, to_other, to_sibling, to_across):
        greet(device)
    peers = 5
    for there, device in (
        (far_to, to_far),
        (far_from, {"frame": f - 2 * toward}),
        (near, to_near),
    ):
        pl.when(there)(functools.partial(greet, device))
        peers = peers + jnp.where(there, 1, 0)

    loads[0].wait()
    loads[1].wait()
    wide = tokens_ref[...].astype(jnp.float32)
    factor = lax.rsqrt(jnp.mean(wide * wide, axis=-1, keepdims=True) + EPS)
    xn[0] = (wide * factor * ngain_ref[...]).astype(jnp.bfloat16)

    pl.semaphore_wait(barrier, peers)

    sent = []

    def send(src, dst, sems, index, device, keep=True):
        copy = pltpu.make_async_remote_copy(
            src_ref=src,
            dst_ref=dst,
            send_sem=sems[0].at[index],
            recv_sem=sems[1].at[index],
            device_id=device,
            device_id_type=MESH,
        )
        if keep:
            sent.append(copy)
        return copy

    def rows_of(p):
        return pl.ds(p * piece, piece)

    ag = (ag_s, ag_r)
    a_right, a_left, b_other, f_ward, c_right, c_left, d_other = [], [], [], [], [], [], []
    for p in range(PIECES):
        r = rows_of(p)
        n = 7 * p
        a_right.append(send(xn.at[0, r], xn.at[2, r], ag, n, to_right))
        a_left.append(send(xn.at[0, r], xn.at[3, r], ag, n + 1, to_left))
        b_other.append(send(xn.at[0, r], xn.at[1, r], ag, n + 2, to_other))
        if p % 2:
            f_ward.append(send(xn.at[2, r], xn.at[4, r], ag, n + 3, to_right))
        else:
            f_ward.append(send(xn.at[3, r], xn.at[4, r], ag, n + 3, to_left))
        c_right.append(send(xn.at[1, r], xn.at[5, r], ag, n + 4, to_right))
        c_left.append(send(xn.at[1, r], xn.at[6, r], ag, n + 5, to_left))
        d_other.append(send(xn.at[4, r], xn.at[7, r], ag, n + 6, to_other))

    def normed_heads(section, gain_ref):
        done = []
        for i in range(heads):
            part_i = section[:, i * HD : (i + 1) * HD]
            scale = lax.rsqrt(jnp.mean(part_i * part_i, axis=-1, keepdims=True) + EPS)
            done.append((part_i * scale * gain_ref[...]).astype(jnp.bfloat16))
        return done

    groups = (
        ((0,), 0, rows, 0),
        ((1, 2, 3), 0, rows, 1),
        ((4,), 0, rows, 4),
        ((5, 6, 7), 0, half, 5),
        ((5, 6, 7), half, half, 8),
    )
    kinds = 4
    copies = 11

    def gathered(group):
        slots, low, count, _ = group
        block = xn[slots[0] : slots[-1] + 1, low : low + count]
        return block.reshape(len(slots) * count, block.shape[-1])

    def kv_copies(group, kind):
        slots, low, count, first = group
        into = (BAND - toward, BAND - 2 * toward, BAND + toward, BAND - 2 * toward)[kind]
        out = BAND - toward if kind == 3 else BAND
        device = (to_sibling, to_far, to_near, to_sibling)[kind]
        r = pl.ds(low, count)
        return [
            send(
                kv.at[out * 8 + PLACE[slot], r],
                kv.at[into * 8 + PLACE[slot], r],
                (kv_s, kv_r),
                kind * copies + first + i,
                device,
                keep=False,
            )
            for i, slot in enumerate(slots)
        ]

    def start_all(some):
        for copy in some:
            copy.start()

    def project_pairs(group):
        slots, low, count, _ = group
        block = gathered(group)
        keys = jnp.dot(block, wk[...], preferred_element_type=jnp.float32)
        pieces = normed_heads(keys, kgain_ref)
        values = jnp.dot(block, wv[...], preferred_element_type=jnp.float32).astype(jnp.bfloat16)
        for n, slot in enumerate(slots):
            at = BAND * 8 + PLACE[slot]
            for i in range(heads):
                kv[at, low : low + count, i * HD : (i + 1) * HD] = pieces[i][
                    n * count : (n + 1) * count
                ]
            kv[at, low : low + count, width:] = values[n * count : (n + 1) * count]
        start_all(kv_copies(group, 0))
        pl.when(far_to)(lambda: start_all(kv_copies(group, 1)))
        pl.when(near)(lambda: start_all(kv_copies(group, 2)))

    def project_queries(group):
        slots, low, count, _ = group
        queries = jnp.dot(gathered(group), wq[...], preferred_element_type=jnp.float32)
        pieces = normed_heads(queries, qgain_ref)
        for n, slot in enumerate(slots):
            for i in range(heads):
                q[PLACE[slot], low : low + count, i * HD : (i + 1) * HD] = pieces[i][
                    n * count : (n + 1) * count
                ]

    def relay(group):
        @pl.when(near)
        def _():
            for came, on in zip(kv_copies(group, 2), kv_copies(group, 3)):
                came.wait_recv()
                on.start()

    for p in range(PIECES):
        a_right[(1, 3, 0, 2)[p]].start()
        a_left[p if p in (0, 3) else 3 - p].start()
        b_other[p].start()

    share = width // 2
    wo_send = send(
        wo_hbm.at[pl.ds(core * share, share)],
        wo.at[pl.ds(width + core * share, share)],
        (wo_s, wo_r),
        0,
        to_across,
    )
    wo_pass = send(
        wo.at[pl.ds(width + core * share, share)],
        wo.at[pl.ds(width + core * share, share)],
        (wo_s, wo_r),
        1,
        to_sibling,
    )
    wo_send.start()

    for copy in loads[2:8]:
        copy.wait()
    project_pairs(groups[0])
    loads[8].wait()
    project_queries(groups[0])

    for early, late in ((0, 1), (2, 3)):
        a_right[late].wait_recv()
        f_ward[late].start()
        a_left[early].wait_recv()
        f_ward[early].start()
        for p in (early, late):
            b_other[p].wait_recv()
            c_right[p].start()
            c_left[p].start()
    for p in (0, 2):
        a_right[p].wait_recv()
        a_left[p + 1].wait_recv()
    project_pairs(groups[1])
    relay(groups[0])
    for p in range(PIECES):
        f_ward[p].wait_recv()
        d_other[p].start()
    project_queries(groups[1])
    project_pairs(groups[2])
    relay(groups[1])
    project_queries(groups[2])
    for late in range(2):
        for p in (2 * late, 2 * late + 1):
            c_right[p].wait_recv()
            c_left[p].wait_recv()
            d_other[p].wait_recv()
        project_pairs(groups[3 + late])
        relay(groups[2 + late])
        project_queries(groups[3 + late])
    loads[9].wait()
    wo_send.wait_recv()
    wo_pass.start()
    relay(groups[4])

    for group in groups:
        for copy in kv_copies(group, 0):
            copy.wait_recv()

        @pl.when(far_from)
        def _():
            for copy in kv_copies(group, 1):
                copy.wait_recv()

        @pl.when(far_to)
        def _():
            for copy in kv_copies(group, 3):
                copy.wait_recv()

    score_factor = 1.0 / HD**0.5

    def attend(k):
        block = (x + k) % 4
        queries = q[2 * k : 2 * k + 2].reshape(BLK, width)
        listed = counts_ref[block]
        weighted = [jnp.zeros((BLK, HD), jnp.float32) for _ in range(heads)]
        totals = [jnp.zeros((BLK, 1), jnp.float32) for _ in range(heads)]
        for m in range(MAXB):
            live = m < listed
            picked = jnp.where(live, lists_ref[block, m], f * NB + block)
            slot = jnp.clip(picked // NB - f + BAND, 0, 2 * BAND)
            spot = slot * NB + (picked % NB - x + 4) % 4
            pair = kv[pl.ds(spot * 2, 2)].reshape(BLK, 2 * width)
            on = jnp.where(live, 1.0, 0.0).astype(jnp.float32)
            for i in range(heads):
                scores = lax.dot_general(
                    queries[:, i * HD : (i + 1) * HD],
                    pair[:, i * HD : (i + 1) * HD],
                    (((1,), (1,)), ((), ())),
                    preferred_element_type=jnp.float32,
                )
                weight = jnp.exp(scores * score_factor) * on
                totals[i] = totals[i] + jnp.sum(weight, axis=-1, keepdims=True)
                weighted[i] = weighted[i] + jnp.dot(
                    weight.astype(jnp.bfloat16),
                    pair[:, width + i * HD : width + (i + 1) * HD],
                    preferred_element_type=jnp.float32,
                )
        for i in range(heads):
            done = (weighted[i] / totals[i]).astype(jnp.bfloat16)
            ctx[k, 0, :, i * HD : (i + 1) * HD] = done[0:rows]
            ctx[k, 1, :, i * HD : (i + 1) * HD] = done[rows:]

    ctx_sends = [
        send(ctx.at[k, 1], ctx.at[k, 2], (ctx_s, ctx_r), k, to_other) for k in range(4)
    ]

    def out_project(k):
        partial = jnp.dot(ctx[k, 0], wo[0:width], preferred_element_type=jnp.float32)
        partial = partial + jnp.dot(ctx[k, 2], wo[width:], preferred_element_type=jnp.float32)
        part[k] = partial.astype(jnp.bfloat16)

    rs = (rs_s, rs_r)
    h_left, h_right, c_l, c_r = [], [], [], []
    for p in range(PIECES):
        r = rows_of(p)
        if p < PIECES // 2:
            h_left.append(send(part.at[2, r], got_h.at[r], rs, 3 * p, to_left))
        else:
            h_right.append(send(part.at[2, r], got_h.at[r], rs, 3 * p, to_right))
        c_l.append(send(part.at[3, r], got_c.at[0, r], rs, 3 * p + 1, to_left))
        c_r.append(send(part.at[1, r], got_c.at[1, r], rs, 3 * p + 2, to_right))

    for k in (2, 3, 1, 0):
        attend(k)
        ctx_sends[k].start()

    wo_pass.wait_recv()
    ctx_sends[2].wait_recv()
    out_project(2)
    for p in range(2):
        h_left[p].start()
        h_right[p].start()
    ctx_sends[3].wait_recv()
    out_project(3)
    c_l[2].start()
    c_l[3].start()
    ctx_sends[1].wait_recv()
    out_project(1)
    c_r[0].start()
    c_r[1].start()
    ctx_sends[0].wait_recv()
    out_project(0)

    def add_in(k, p):
        r = slice(p * piece, (p + 1) * piece)
        total = part[k, r].astype(jnp.float32) + got_h[r].astype(jnp.float32)
        part[k, r] = total.astype(jnp.bfloat16)

    for p in range(2):
        h_left[p].wait_recv()
        add_in(3, p)
        c_l[p].start()
        h_right[p].wait_recv()
        add_in(1, p + 2)
        c_r[p + 2].start()
    for p in (2, 3, 0, 1):
        r = slice(p * piece, (p + 1) * piece)
        c_l[p].wait_recv()
        c_r[(p + 2) % 4].wait_recv()
    total = part[0].astype(jnp.float32) + got_c[0].astype(jnp.float32)
    out_ref[...] = (total + got_c[1].astype(jnp.float32)).astype(jnp.bfloat16)

    for copy in sent:
        copy.wait_send()
    for kind, there in enumerate((None, far_to, near, near)):

        def finish():
            for group in groups:
                for copy in kv_copies(group, kind):
                    copy.wait_send()

        if there is None:
            finish()
        else:
            pl.when(there)(finish)


def per_device(
    tokens,
    norm_gain,
    w_query,
    w_key,
    w_value,
    query_gain,
    key_gain,
    w_out,
    block_lists,
    block_counts,
):
    rows, depth = tokens.shape
    width = w_query.shape[1]
    dma = pltpu.SemaphoreType.DMA
    bf16 = jnp.bfloat16
    hbm = pl.BlockSpec(memory_space=pltpu.HBM)
    return pl.pallas_call(
        functools.partial(kernel, lax.axis_size("frame")),
        out_shape=jax.ShapeDtypeStruct((rows, depth), bf16),
        in_specs=[hbm] * 10,
        out_specs=pl.BlockSpec(memory_space=pltpu.VMEM),
        scratch_shapes=[
            pltpu.VMEM((rows, depth), bf16),
            pltpu.VMEM((1, depth), jnp.float32),
            pltpu.VMEM((1, HD), jnp.float32),
            pltpu.VMEM((1, HD), jnp.float32),
            pltpu.SMEM(block_lists.shape, jnp.int32),
            pltpu.SMEM(block_counts.shape, jnp.int32),
            pltpu.VMEM((depth, width), bf16),
            pltpu.VMEM((depth, width), bf16),
            pltpu.VMEM((depth, width), bf16),
            pltpu.VMEM((2 * width, depth), bf16),
            pltpu.VMEM((8, rows, depth), bf16),
            pltpu.VMEM((8, rows, width), bf16),
            pltpu.VMEM(((2 * BAND + 1) * 8, rows, 2 * width), bf16),
            pltpu.VMEM((4, 3, rows, width), bf16),
            pltpu.VMEM((4, rows, depth), bf16),
            pltpu.VMEM((rows, depth), bf16),
            pltpu.VMEM((2, rows, depth), bf16),
            dma((10,)),
            dma((7 * PIECES,)),
            dma((7 * PIECES,)),
            dma((44,)),
            dma((44,)),
            dma((2,)),
            dma((2,)),
            dma((4,)),
            dma((4,)),
            dma((3 * PIECES,)),
            dma((3 * PIECES,)),
        ],
        compiler_params=pltpu.CompilerParams(
            collective_id=0, has_side_effects=True, vmem_limit_bytes=63 * 1024 * 1024
        ),
    )(
        tokens,
        norm_gain.reshape(1, depth),
        query_gain.reshape(1, HD),
        key_gain.reshape(1, HD),
        block_lists,
        block_counts,
        w_query,
        w_key,
        w_value,
        w_out,
    )


def solution(mesh):
    placed = (
        P(("frame", "head"), None),
        P(),
        P(None, "head"),
        P(None, "head"),
        P(None, "head"),
        P(),
        P(),
        P("head", None),
        P("frame", None),
        P("frame"),
    )
    return jax.shard_map(
        per_device,
        mesh=mesh,
        in_specs=placed,
        out_specs=P(("frame", "head"), None),
        check_vma=False,
    )
```

```python
import functools

import jax
import jax.numpy as jnp
from jax import lax
from jax.experimental import pallas as pl
from jax.experimental.pallas import tpu as pltpu
from jax.sharding import PartitionSpec as P

HD = 128
BLK = 128
MAXB = 6
BAND = 2
NB = 4
EPS = 1e-06
PIECES = 4
MESH = pl.DeviceIdType.MESH

SLOT = (0, 2, 1, 3)


def kernel(
    frames,
    tokens_hbm,
    ngain_hbm,
    qgain_hbm,
    kgain_hbm,
    lists_hbm,
    counts_hbm,
    wq_hbm,
    wk_hbm,
    wv_hbm,
    wo_hbm,
    own_hbm,
    from_right_hbm,
    from_left_hbm,
    tokens_ref,
    ngain_ref,
    qgain_ref,
    kgain_ref,
    lists_ref,
    counts_ref,
    wq,
    wk,
    wv,
    wo,
    xn,
    q,
    kv,
    ctx,
    part,
    got_h,
    in_sem,
    ag_s,
    ag_r,
    kv_s,
    kv_r,
    wo_s,
    wo_r,
    ctx_s,
    ctx_r,
    rs_s,
    rs_r,
):
    f = lax.axis_index("frame")
    head = lax.axis_index("head")
    x, y = head // 2, head % 2
    core = f % 2
    toward = 1 - 2 * core
    right, left = (x + 1) % 4, (x + 3) % 4
    to_right, to_left = {"head": right * 2 + y}, {"head": left * 2 + y}
    to_other = {"head": x * 2 + 1 - y}
    to_sibling = {"frame": f + toward}
    to_far = {"frame": f + 2 * toward}
    to_near = {"frame": f - toward}
    to_across = {"frame": (f + frames // 2) % frames, "head": x * 2 + 1 - y}
    rows = tokens_ref.shape[0]
    half, piece = rows // 2, rows // PIECES
    width = wq.shape[1]
    heads = width // HD

    def within(d):
        return jnp.logical_and(f + d >= 0, f + d < frames)

    far_to, far_from, near = within(2 * toward), within(-2 * toward), within(-toward)
    mid = frames // 2
    crossing = jnp.logical_or(
        jnp.logical_and(f == mid - 1, core == 1), jnp.logical_and(f == mid, core == 0)
    )
    close = jnp.logical_and(near, jnp.logical_not(crossing))
    by_way = jnp.logical_not(far_to)
    to_way = {"frame": f - toward * (mid - 1)}
    from_way = {"frame": f + toward * (mid - 2)}
    to_crossing = {"frame": f - toward * (mid - 2)}

    loads = [
        pltpu.make_async_copy(src, dst, in_sem.at[i])
        for i, (src, dst) in enumerate(
            (
                (tokens_hbm, tokens_ref),
                (ngain_hbm, ngain_ref),
                (qgain_hbm, qgain_ref),
                (kgain_hbm, kgain_ref),
                (lists_hbm, lists_ref),
                (counts_hbm, counts_ref),
                (wk_hbm, wk),
                (wv_hbm, wv),
                (wq_hbm, wq),
                (wo_hbm, wo.at[0:width]),
            )
        )
    ]
    loads[0].start()
    loads[1].start()

    barrier = pltpu.get_barrier_semaphore()

    def greet(device):
        pl.semaphore_signal(barrier, inc=1, device_id=device, device_id_type=MESH)

    for device in (to_right, to_left, to_other, to_sibling, to_across):
        greet(device)
    peers = 5
    for there, device in (
        (far_to, to_far),
        (far_from, {"frame": f - 2 * toward}),
        (close, to_near),
        (crossing, to_way),
        (crossing, from_way),
        (by_way, to_way),
        (by_way, to_crossing),
    ):
        pl.when(there)(functools.partial(greet, device))
        peers = peers + jnp.where(there, 1, 0)

    loads[0].wait()
    loads[1].wait()
    for copy in loads[2:]:
        copy.start()
    wide = tokens_ref[...].astype(jnp.float32)
    factor = lax.rsqrt(jnp.mean(wide * wide, axis=-1, keepdims=True) + EPS)
    xn[0] = (wide * factor * ngain_ref[...]).astype(jnp.bfloat16)

    pl.semaphore_wait(barrier, peers)

    sent = []

    def send(src, dst, sems, index, device, keep=True):
        copy = pltpu.make_async_remote_copy(
            src_ref=src,
            dst_ref=dst,
            send_sem=sems[0].at[index],
            recv_sem=sems[1].at[index],
            device_id=device,
            device_id_type=MESH,
        )
        if keep:
            sent.append(copy)
        return copy

    def rows_of(p):
        return pl.ds(p * piece, piece)

    ag = (ag_s, ag_r)
    a_right, a_left, b_other, f_ward, c_right, c_left, d_other = [], [], [], [], [], [], []
    for p in range(PIECES):
        r = rows_of(p)
        n = 7 * p
        a_right.append(send(xn.at[0, r], xn.at[3, r], ag, n, to_right))
        a_left.append(send(xn.at[0, r], xn.at[2, r], ag, n + 1, to_left))
        b_other.append(send(xn.at[0, r], xn.at[4, r], ag, n + 2, to_other))
        if p % 2:
            f_ward.append(send(xn.at[3, r], xn.at[1, r], ag, n + 3, to_right))
        else:
            f_ward.append(send(xn.at[2, r], xn.at[1, r], ag, n + 3, to_left))
        c_right.append(send(xn.at[4, r], xn.at[7, r], ag, n + 4, to_right))
        c_left.append(send(xn.at[4, r], xn.at[6, r], ag, n + 5, to_left))
        d_other.append(send(xn.at[1, r], xn.at[5, r], ag, n + 6, to_other))

    def normed_heads(section, gain_ref):
        done = []
        for i in range(heads):
            part_i = section[:, i * HD : (i + 1) * HD]
            scale = lax.rsqrt(jnp.mean(part_i * part_i, axis=-1, keepdims=True) + EPS)
            done.append((part_i * scale * gain_ref[...]).astype(jnp.bfloat16))
        return done

    groups = (
        (0, 1, 0, rows),
        (2, 3, 0, rows),
        (1, 1, 0, rows),
        (5, 3, 0, half),
        (5, 3, half, piece),
        (5, 3, half + piece, piece),
    )

    def gathered(group):
        slot, count, low, each = groups[group]
        block = xn[slot : slot + count, low : low + each]
        return block.reshape(count * each, block.shape[-1])

    def kv_copy(group, kind):
        slot, count, low, each = groups[group]
        out, into, device, send_kind, recv_kind = (
            (BAND, BAND - toward, to_sibling, 0, 0),
            (BAND, BAND - 2 * toward, to_far, 1, 1),
            (BAND, BAND + toward, to_near, 2, 2),
            (BAND - toward, BAND - 2 * toward, to_sibling, 3, 3),
            (BAND, BAND - 2 * toward, to_way, 2, 3),
            (BAND + 2 * toward, BAND - toward, to_crossing, 1, 2),
        )[kind]
        r = pl.ds(low, each)
        return pltpu.make_async_remote_copy(
            src_ref=kv.at[pl.ds(out * 8 + slot, count), r],
            dst_ref=kv.at[pl.ds(into * 8 + slot, count), r],
            send_sem=kv_s.at[send_kind * len(groups) + group],
            recv_sem=kv_r.at[recv_kind * len(groups) + group],
            device_id=device,
            device_id_type=MESH,
        )

    def project_pairs(group):
        slot, count, low, each = groups[group]
        block = gathered(group)
        keys = jnp.dot(block, wk[...], preferred_element_type=jnp.float32)
        pieces = normed_heads(keys, kgain_ref)
        values = jnp.dot(block, wv[...], preferred_element_type=jnp.float32).astype(jnp.bfloat16)
        for n in range(count):
            at, r = BAND * 8 + slot + n, slice(n * each, (n + 1) * each)
            for i in range(heads):
                kv[at, low : low + each, i * HD : (i + 1) * HD] = pieces[i][r]
            kv[at, low : low + each, width:] = values[r]
        pl.when(close)(lambda: kv_copy(group, 2).start())
        pl.when(crossing)(lambda: kv_copy(group, 4).start())
        pl.when(far_to)(lambda: kv_copy(group, 1).start())
        kv_copy(group, 0).start()

    def project_queries(group):
        slot, count, low, each = groups[group]
        queries = jnp.dot(gathered(group), wq[...], preferred_element_type=jnp.float32)
        pieces = normed_heads(queries, qgain_ref)
        for n in range(count):
            for i in range(heads):
                q[slot + n, low : low + each, i * HD : (i + 1) * HD] = pieces[i][
                    n * each : (n + 1) * each
                ]

    def pass_on(group):
        @pl.when(by_way)
        def _():
            kv_copy(group, 3).wait_recv()
            kv_copy(group, 5).start()

    def relay(group):
        @pl.when(near)
        def _():
            kv_copy(group, 2).wait_recv()
            kv_copy(group, 3).start()

    for p in range(PIECES):
        a_right[(1, 3, 0, 2)[p]].start()
        a_left[p if p in (0, 3) else 3 - p].start()
        b_other[p].start()

    share = width // 2
    wo_send = send(
        wo_hbm.at[pl.ds(core * share, share)],
        wo.at[pl.ds(width + core * share, share)],
        (wo_s, wo_r),
        0,
        to_across,
    )
    wo_pass = send(
        wo.at[pl.ds(width + core * share, share)],
        wo.at[pl.ds(width + core * share, share)],
        (wo_s, wo_r),
        1,
        to_sibling,
    )
    wo_send.start()

    for copy in loads[2:8]:
        copy.wait()
    project_pairs(0)
    loads[8].wait()
    project_queries(0)

    for early, late in ((0, 1), (2, 3)):
        a_right[late].wait_recv()
        f_ward[late].start()
        a_left[early].wait_recv()
        f_ward[early].start()
        for p in (early, late):
            b_other[p].wait_recv()
            c_right[p].start()
            c_left[p].start()
    for p in (0, 2):
        a_right[p].wait_recv()
        a_left[p + 1].wait_recv()
    project_pairs(1)
    for p in range(PIECES):
        f_ward[p].wait_recv()
        d_other[p].start()
    pass_on(0)
    project_queries(1)
    project_pairs(2)
    relay(0)
    project_queries(2)
    pass_on(1)
    for first, last, group in ((0, 2, 3), (2, 3, 4), (3, 4, 5)):
        for p in range(first, last):
            c_right[p].wait_recv()
            c_left[p].wait_recv()
            d_other[p].wait_recv()
        project_pairs(group)
        pass_on(group - 1)
        if group < 5:
            project_queries(group)
            relay(group - 2)
    project_queries(5)
    loads[9].wait()
    wo_send.wait_recv()
    wo_pass.start()
    pass_on(5)
    for group in (3, 4, 5):
        relay(group)

    for group in range(len(groups)):
        kv_copy(group, 0).wait_recv()

        @pl.when(far_from)
        def _():
            kv_copy(group, 1).wait_recv()

        @pl.when(far_to)
        def _():
            kv_copy(group, 3).wait_recv()

    score_factor = 1.0 / HD**0.5

    def attend(k):
        block = (x + k) % 4
        own = SLOT[k]
        queries = jnp.concatenate([q[own], q[own + 4]], axis=0)
        listed = counts_ref[block]
        pairs, on = [], []
        for m in range(MAXB):
            live = m < listed
            picked = jnp.where(live, lists_ref[block, m], f * NB + block)
            frame = jnp.clip(picked // NB - f + BAND, 0, 2 * BAND)
            across = (picked % NB - x + 4) % 4
            spot = frame * 8 + (across % 2) * 2 + across // 2
            pairs += [kv[spot], kv[spot + 4]]
            on.append(jnp.where(live, 1.0, 0.0).astype(jnp.float32))
        weighted, totals = [], []
        for i in range(heads):
            keys = jnp.concatenate([pair[:, i * HD : (i + 1) * HD] for pair in pairs], axis=0)
            values = jnp.concatenate(
                [pair[:, width + i * HD : width + (i + 1) * HD] for pair in pairs], axis=0
            )
            scores = lax.dot_general(
                queries[:, i * HD : (i + 1) * HD],
                keys,
                (((1,), (1,)), ((), ())),
                preferred_element_type=jnp.float32,
            )
            weights = [
                jnp.exp(scores[:, m * BLK : (m + 1) * BLK] * score_factor) * on[m]
                for m in range(MAXB)
            ]
            summed = functools.reduce(jnp.add, weights)
            totals.append(jnp.sum(summed, axis=-1, keepdims=True))
            rounded = jnp.concatenate([weight.astype(jnp.bfloat16) for weight in weights], axis=1)
            weighted.append(jnp.dot(rounded, values, preferred_element_type=jnp.float32))
        for i in range(heads):
            done = (weighted[i] / totals[i]).astype(jnp.bfloat16)
            ctx[k, 0, :, i * HD : (i + 1) * HD] = done[0:rows]
            ctx[k, 1, :, i * HD : (i + 1) * HD] = done[rows:]

    ctx_sends = [
        send(ctx.at[k, 1], ctx.at[k, 2], (ctx_s, ctx_r), k, to_other) for k in range(4)
    ]

    def out_project(k):
        partial = jnp.dot(ctx[k, 0], wo[0:width], preferred_element_type=jnp.float32)
        partial = partial + jnp.dot(ctx[k, 2], wo[width:], preferred_element_type=jnp.float32)
        part[k] = partial.astype(jnp.bfloat16)

    rs = (rs_s, rs_r)
    h_left, h_right, c_l, c_r = [], [], [], []
    for p in range(PIECES):
        r = rows_of(p)
        if p < PIECES // 2:
            h_left.append(send(part.at[2, r], got_h.at[r], rs, 3 * p, to_left))
        else:
            h_right.append(send(part.at[2, r], got_h.at[r], rs, 3 * p, to_right))
        c_l.append(send(part.at[3, r], from_right_hbm.at[r], rs, 3 * p + 1, to_left))
        c_r.append(send(part.at[1, r], from_left_hbm.at[r], rs, 3 * p + 2, to_right))

    for k in (2, 3, 1):
        attend(k)
        ctx_sends[k].start()
    wo_pass.wait_recv()
    ctx_sends[2].wait_recv()
    out_project(2)
    for p in range(2):
        h_left[p].start()
        h_right[p].start()
    attend(0)
    ctx_sends[0].start()
    ctx_sends[3].wait_recv()
    out_project(3)
    c_l[2].start()
    c_l[3].start()
    ctx_sends[1].wait_recv()
    out_project(1)
    c_r[0].start()
    c_r[1].start()

    def add_in(k, p):
        r = slice(p * piece, (p + 1) * piece)
        total = part[k, r].astype(jnp.float32) + got_h[r].astype(jnp.float32)
        part[k, r] = total.astype(jnp.bfloat16)

    for p in range(2):
        h_left[p].wait_recv()
        add_in(3, p)
        c_l[p].start()
        h_right[p].wait_recv()
        add_in(1, p + 2)
        c_r[p + 2].start()
    ctx_sends[0].wait_recv()
    out_project(0)
    mine = pltpu.make_async_copy(part.at[0], own_hbm, in_sem.at[0])
    mine.start()
    for p in (2, 3, 0, 1):
        c_l[p].wait_recv()
        c_r[(p + 2) % 4].wait_recv()
    mine.wait()

    for copy in sent:
        copy.wait_send()
    for kind, there in ((0, None), (1, far_to), (2, close), (3, near), (4, crossing), (5, by_way)):

        def finish():
            for group in range(len(groups)):
                kv_copy(group, kind).wait_send()

        if there is None:
            finish()
        else:
            pl.when(there)(finish)


def per_device(
    tokens,
    norm_gain,
    w_query,
    w_key,
    w_value,
    query_gain,
    key_gain,
    w_out,
    block_lists,
    block_counts,
):
    rows, depth = tokens.shape
    width = w_query.shape[1]
    dma = pltpu.SemaphoreType.DMA
    bf16 = jnp.bfloat16
    hbm = pl.BlockSpec(memory_space=pltpu.HBM)
    terms = pl.pallas_call(
        functools.partial(kernel, lax.axis_size("frame")),
        out_shape=[jax.ShapeDtypeStruct((rows, depth), bf16)] * 3,
        in_specs=[hbm] * 10,
        out_specs=[hbm] * 3,
        scratch_shapes=[
            pltpu.VMEM((rows, depth), bf16),
            pltpu.VMEM((1, depth), jnp.float32),
            pltpu.VMEM((1, HD), jnp.float32),
            pltpu.VMEM((1, HD), jnp.float32),
            pltpu.SMEM(block_lists.shape, jnp.int32),
            pltpu.SMEM(block_counts.shape, jnp.int32),
            pltpu.VMEM((depth, width), bf16),
            pltpu.VMEM((depth, width), bf16),
            pltpu.VMEM((depth, width), bf16),
            pltpu.VMEM((2 * width, depth), bf16),
            pltpu.VMEM((8, rows, depth), bf16),
            pltpu.VMEM((8, rows, width), bf16),
            pltpu.VMEM(((2 * BAND + 1) * 8, rows, 2 * width), bf16),
            pltpu.VMEM((4, 3, rows, width), bf16),
            pltpu.VMEM((4, rows, depth), bf16),
            pltpu.VMEM((rows, depth), bf16),
            dma((10,)),
            dma((7 * PIECES,)),
            dma((7 * PIECES,)),
            dma((24,)),
            dma((24,)),
            dma((2,)),
            dma((2,)),
            dma((4,)),
            dma((4,)),
            dma((3 * PIECES,)),
            dma((3 * PIECES,)),
        ],
        compiler_params=pltpu.CompilerParams(
            collective_id=0, has_side_effects=True, vmem_limit_bytes=63 * 1024 * 1024
        ),
    )(
        tokens,
        norm_gain.reshape(1, depth),
        query_gain.reshape(1, HD),
        key_gain.reshape(1, HD),
        block_lists,
        block_counts,
        w_query,
        w_key,
        w_value,
        w_out,
    )
    own, from_right, from_left = (term.astype(jnp.float32) for term in terms)
    return (own + from_right + from_left).astype(bf16)


def solution(mesh):
    placed = (
        P(("frame", "head"), None),
        P(),
        P(None, "head"),
        P(None, "head"),
        P(None, "head"),
        P(),
        P(),
        P("head", None),
        P("frame", None),
        P("frame"),
    )
    return jax.shard_map(
        per_device,
        mesh=mesh,
        in_specs=placed,
        out_specs=P(("frame", "head"), None),
        check_vma=False,
    )
```

```python
import functools

import jax
import jax.numpy as jnp
from jax import lax
from jax.experimental import pallas as pl
from jax.experimental.pallas import tpu as pltpu
from jax.sharding import PartitionSpec as P

HD = 128
BLK = 128
MAXB = 6
BAND = 2
NB = 4
EPS = 1e-06
PIECES = 4
BY_WAY = 2
MESH = pl.DeviceIdType.MESH

SLOT = (0, 2, 1, 3)


def kernel(
    frames,
    tokens_hbm,
    ngain_hbm,
    qgain_hbm,
    kgain_hbm,
    lists_hbm,
    counts_hbm,
    wq_hbm,
    wk_hbm,
    wv_hbm,
    wo_hbm,
    own_hbm,
    from_right_hbm,
    from_left_hbm,
    tokens_ref,
    ngain_ref,
    qgain_ref,
    kgain_ref,
    lists_ref,
    counts_ref,
    wq,
    wk,
    wv,
    wo,
    xn,
    q,
    kv,
    ctx,
    part,
    got_h,
    in_sem,
    ag_s,
    ag_r,
    kv_s,
    kv_r,
    wo_s,
    wo_r,
    ctx_s,
    ctx_r,
    rs_s,
    rs_r,
):
    f = lax.axis_index("frame")
    head = lax.axis_index("head")
    x, y = head // 2, head % 2
    core = f % 2
    toward = 1 - 2 * core
    right, left = (x + 1) % 4, (x + 3) % 4
    to_right, to_left = {"head": right * 2 + y}, {"head": left * 2 + y}
    to_other = {"head": x * 2 + 1 - y}
    to_sibling = {"frame": f + toward}
    to_far = {"frame": f + 2 * toward}
    to_near = {"frame": f - toward}
    to_across = {"frame": (f + frames // 2) % frames, "head": x * 2 + 1 - y}
    rows = tokens_ref.shape[0]
    half, piece = rows // 2, rows // PIECES
    width = wq.shape[1]
    heads = width // HD

    def within(d):
        return jnp.logical_and(f + d >= 0, f + d < frames)

    far_to, far_from, near = within(2 * toward), within(-2 * toward), within(-toward)
    mid = frames // 2
    crossing = jnp.logical_or(
        jnp.logical_and(f == mid - 1, core == 1), jnp.logical_and(f == mid, core == 0)
    )
    close = jnp.logical_and(near, jnp.logical_not(crossing))
    by_way = jnp.logical_not(far_to)
    to_way = {"frame": f - toward * (mid - 1)}
    from_way = {"frame": f + toward * (mid - 2)}
    to_crossing = {"frame": f - toward * (mid - 2)}

    loads = [
        pltpu.make_async_copy(src, dst, in_sem.at[i])
        for i, (src, dst) in enumerate(
            (
                (tokens_hbm, tokens_ref),
                (ngain_hbm, ngain_ref),
                (qgain_hbm, qgain_ref),
                (kgain_hbm, kgain_ref),
                (lists_hbm, lists_ref),
                (counts_hbm, counts_ref),
                (wk_hbm, wk),
                (wv_hbm, wv),
                (wq_hbm, wq),
                (wo_hbm, wo.at[0:width]),
            )
        )
    ]
    loads[0].start()
    loads[1].start()

    barrier = pltpu.get_barrier_semaphore()

    def greet(device):
        pl.semaphore_signal(barrier, inc=1, device_id=device, device_id_type=MESH)

    for device in (to_right, to_left, to_other, to_sibling, to_across):
        greet(device)
    peers = 5
    for there, device in (
        (far_to, to_far),
        (far_from, {"frame": f - 2 * toward}),
        (near, to_near),
        (crossing, to_way),
        (crossing, from_way),
        (by_way, to_way),
        (by_way, to_crossing),
    ):
        pl.when(there)(functools.partial(greet, device))
        peers = peers + jnp.where(there, 1, 0)

    loads[0].wait()
    loads[1].wait()
    for copy in loads[2:]:
        copy.start()
    wide = tokens_ref[...].astype(jnp.float32)
    factor = lax.rsqrt(jnp.mean(wide * wide, axis=-1, keepdims=True) + EPS)
    xn[0] = (wide * factor * ngain_ref[...]).astype(jnp.bfloat16)

    pl.semaphore_wait(barrier, peers)

    sent = []

    def send(src, dst, sems, index, device, keep=True):
        copy = pltpu.make_async_remote_copy(
            src_ref=src,
            dst_ref=dst,
            send_sem=sems[0].at[index],
            recv_sem=sems[1].at[index],
            device_id=device,
            device_id_type=MESH,
        )
        if keep:
            sent.append(copy)
        return copy

    def rows_of(p):
        return pl.ds(p * piece, piece)

    ag = (ag_s, ag_r)
    a_right, a_left, b_other, f_ward, c_right, c_left, d_other = [], [], [], [], [], [], []
    for p in range(PIECES):
        r = rows_of(p)
        n = 7 * p
        a_right.append(send(xn.at[0, r], xn.at[3, r], ag, n, to_right))
        a_left.append(send(xn.at[0, r], xn.at[2, r], ag, n + 1, to_left))
        b_other.append(send(xn.at[0, r], xn.at[4, r], ag, n + 2, to_other))
        if p % 2:
            f_ward.append(send(xn.at[3, r], xn.at[1, r], ag, n + 3, to_right))
        else:
            f_ward.append(send(xn.at[2, r], xn.at[1, r], ag, n + 3, to_left))
        c_right.append(send(xn.at[4, r], xn.at[7, r], ag, n + 4, to_right))
        c_left.append(send(xn.at[4, r], xn.at[6, r], ag, n + 5, to_left))
        d_other.append(send(xn.at[1, r], xn.at[5, r], ag, n + 6, to_other))

    def normed_heads(section, gain_ref):
        done = []
        for i in range(heads):
            part_i = section[:, i * HD : (i + 1) * HD]
            scale = lax.rsqrt(jnp.mean(part_i * part_i, axis=-1, keepdims=True) + EPS)
            done.append((part_i * scale * gain_ref[...]).astype(jnp.bfloat16))
        return done

    groups = (
        (0, 1, 0, rows),
        (2, 3, 0, rows),
        (1, 1, 0, rows),
        (5, 3, 0, half),
        (5, 3, half, piece),
        (5, 3, half + piece, piece),
    )

    def gathered(group):
        slot, count, low, each = groups[group]
        block = xn[slot : slot + count, low : low + each]
        return block.reshape(count * each, block.shape[-1])

    def kv_copy(group, kind):
        slot, count, low, each = groups[group]
        out, into, device, send_kind, recv_kind = (
            (BAND, BAND - toward, to_sibling, 0, 0),
            (BAND, BAND - 2 * toward, to_far, 1, 1),
            (BAND, BAND + toward, to_near, 2, 2),
            (BAND - toward, BAND - 2 * toward, to_sibling, 3, 3),
            (BAND, BAND - 2 * toward, to_way, 2, 3),
            (BAND + 2 * toward, BAND - toward, to_crossing, 1, 2),
        )[kind]
        r = pl.ds(low, each)
        return pltpu.make_async_remote_copy(
            src_ref=kv.at[pl.ds(out * 8 + slot, count), r],
            dst_ref=kv.at[pl.ds(into * 8 + slot, count), r],
            send_sem=kv_s.at[send_kind * len(groups) + group],
            recv_sem=kv_r.at[recv_kind * len(groups) + group],
            device_id=device,
            device_id_type=MESH,
        )

    def project_pairs(group):
        slot, count, low, each = groups[group]
        block = gathered(group)
        keys = jnp.dot(block, wk[...], preferred_element_type=jnp.float32)
        pieces = normed_heads(keys, kgain_ref)
        values = jnp.dot(block, wv[...], preferred_element_type=jnp.float32).astype(jnp.bfloat16)
        for n in range(count):
            at, r = BAND * 8 + slot + n, slice(n * each, (n + 1) * each)
            for i in range(heads):
                kv[at, low : low + each, i * HD : (i + 1) * HD] = pieces[i][r]
            kv[at, low : low + each, width:] = values[r]
        if group < BY_WAY:
            pl.when(close)(lambda: kv_copy(group, 2).start())
            pl.when(crossing)(lambda: kv_copy(group, 4).start())
        else:
            pl.when(near)(lambda: kv_copy(group, 2).start())
        pl.when(far_to)(lambda: kv_copy(group, 1).start())
        kv_copy(group, 0).start()

    def project_queries(group):
        slot, count, low, each = groups[group]
        queries = jnp.dot(gathered(group), wq[...], preferred_element_type=jnp.float32)
        pieces = normed_heads(queries, qgain_ref)
        for n in range(count):
            for i in range(heads):
                q[slot + n, low : low + each, i * HD : (i + 1) * HD] = pieces[i][
                    n * each : (n + 1) * each
                ]

    def pass_on(group):
        @pl.when(by_way)
        def _():
            kv_copy(group, 3).wait_recv()
            kv_copy(group, 5).start()

    def relay(group, there):
        @pl.when(there)
        def _():
            kv_copy(group, 2).wait_recv()
            kv_copy(group, 3).start()

    for p in range(PIECES):
        a_right[(1, 3, 0, 2)[p]].start()
        a_left[p if p in (0, 3) else 3 - p].start()
        b_other[p].start()

    share = width // 2
    wo_send = send(
        wo_hbm.at[pl.ds(core * share, share)],
        wo.at[pl.ds(width + core * share, share)],
        (wo_s, wo_r),
        0,
        to_across,
    )
    wo_pass = send(
        wo.at[pl.ds(width + core * share, share)],
        wo.at[pl.ds(width + core * share, share)],
        (wo_s, wo_r),
        1,
        to_sibling,
    )
    wo_send.start()

    for copy in loads[2:8]:
        copy.wait()
    project_pairs(0)
    loads[8].wait()
    project_queries(0)

    for early, late in ((0, 1), (2, 3)):
        a_right[late].wait_recv()
        f_ward[late].start()
        a_left[early].wait_recv()
        f_ward[early].start()
        for p in (early, late):
            b_other[p].wait_recv()
            c_right[p].start()
            c_left[p].start()
    for p in (0, 2):
        a_right[p].wait_recv()
        a_left[p + 1].wait_recv()
    project_pairs(1)
    for p in range(PIECES):
        f_ward[p].wait_recv()
        d_other[p].start()
    pass_on(0)
    project_queries(1)
    project_pairs(2)
    project_queries(2)
    relay(0, close)
    for first, last, group in ((0, 2, 3), (2, 3, 4), (3, 4, 5)):
        for p in range(first, last):
            c_right[p].wait_recv()
            c_left[p].wait_recv()
            d_other[p].wait_recv()
        project_pairs(group)
        if group - 2 < BY_WAY:
            pass_on(group - 2)
        if group < 5:
            project_queries(group)
        relay(group - 2, close)
    project_queries(5)
    loads[9].wait()
    wo_send.wait_recv()
    wo_pass.start()
    relay(4, close)
    relay(5, close)
    for group in range(len(groups)):
        relay(group, crossing)

    for group in range(len(groups)):
        kv_copy(group, 0).wait_recv()

        @pl.when(far_from)
        def _():
            kv_copy(group, 1).wait_recv()

        @pl.when(far_to)
        def _():
            kv_copy(group, 3).wait_recv()

    score_factor = 1.0 / HD**0.5

    def attend(k):
        block = (x + k) % 4
        own = SLOT[k]
        queries = jnp.concatenate([q[own], q[own + 4]], axis=0)
        listed = counts_ref[block]
        pairs, on = [], []
        for m in range(MAXB):
            live = m < listed
            picked = jnp.where(live, lists_ref[block, m], f * NB + block)
            frame = jnp.clip(picked // NB - f + BAND, 0, 2 * BAND)
            across = (picked % NB - x + 4) % 4
            spot = frame * 8 + (across % 2) * 2 + across // 2
            pairs += [kv[spot], kv[spot + 4]]
            on.append(jnp.where(live, 1.0, 0.0).astype(jnp.float32))
        weighted, totals = [], []
        for i in range(heads):
            keys = jnp.concatenate([pair[:, i * HD : (i + 1) * HD] for pair in pairs], axis=0)
            values = jnp.concatenate(
                [pair[:, width + i * HD : width + (i + 1) * HD] for pair in pairs], axis=0
            )
            scores = lax.dot_general(
                queries[:, i * HD : (i + 1) * HD],
                keys,
                (((1,), (1,)), ((), ())),
                preferred_element_type=jnp.float32,
            )
            weights = [
                jnp.exp(scores[:, m * BLK : (m + 1) * BLK] * score_factor) * on[m]
                for m in range(MAXB)
            ]
            summed = functools.reduce(jnp.add, weights)
            totals.append(jnp.sum(summed, axis=-1, keepdims=True))
            rounded = jnp.concatenate([weight.astype(jnp.bfloat16) for weight in weights], axis=1)
            weighted.append(jnp.dot(rounded, values, preferred_element_type=jnp.float32))
        for i in range(heads):
            done = (weighted[i] / totals[i]).astype(jnp.bfloat16)
            ctx[k, 0, :, i * HD : (i + 1) * HD] = done[0:rows]
            ctx[k, 1, :, i * HD : (i + 1) * HD] = done[rows:]

    ctx_sends = [
        send(ctx.at[k, 1], ctx.at[k, 2], (ctx_s, ctx_r), k, to_other) for k in range(4)
    ]

    def out_project(k):
        partial = jnp.dot(ctx[k, 0], wo[0:width], preferred_element_type=jnp.float32)
        partial = partial + jnp.dot(ctx[k, 2], wo[width:], preferred_element_type=jnp.float32)
        part[k] = partial.astype(jnp.bfloat16)

    rs = (rs_s, rs_r)
    h_left, h_right, c_l, c_r = [], [], [], []
    for p in range(PIECES):
        r = rows_of(p)
        if p < PIECES // 2:
            h_left.append(send(part.at[2, r], got_h.at[r], rs, 3 * p, to_left))
        else:
            h_right.append(send(part.at[2, r], got_h.at[r], rs, 3 * p, to_right))
        c_l.append(send(part.at[3, r], from_right_hbm.at[r], rs, 3 * p + 1, to_left))
        c_r.append(send(part.at[1, r], from_left_hbm.at[r], rs, 3 * p + 2, to_right))

    for k in (2, 3, 1):
        attend(k)
        ctx_sends[k].start()
    wo_pass.wait_recv()
    ctx_sends[2].wait_recv()
    out_project(2)
    for p in range(2):
        h_left[p].start()
        h_right[p].start()
    attend(0)
    ctx_sends[0].start()
    ctx_sends[3].wait_recv()
    out_project(3)
    c_l[2].start()
    c_l[3].start()
    ctx_sends[1].wait_recv()
    out_project(1)
    c_r[0].start()
    c_r[1].start()

    def add_in(k, p):
        r = slice(p * piece, (p + 1) * piece)
        total = part[k, r].astype(jnp.float32) + got_h[r].astype(jnp.float32)
        part[k, r] = total.astype(jnp.bfloat16)

    for p in range(2):
        h_left[p].wait_recv()
        add_in(3, p)
        c_l[p].start()
        h_right[p].wait_recv()
        add_in(1, p + 2)
        c_r[p + 2].start()
    ctx_sends[0].wait_recv()
    out_project(0)
    mine = pltpu.make_async_copy(part.at[0], own_hbm, in_sem.at[0])
    mine.start()
    for p in (2, 3, 0, 1):
        c_l[p].wait_recv()
        c_r[(p + 2) % 4].wait_recv()
    mine.wait()

    for copy in sent:
        copy.wait_send()
    for group in range(len(groups)):
        detour = group < BY_WAY
        kv_copy(group, 0).wait_send()
        for kind, there in (
            (1, far_to),
            (2, close if detour else near),
            (3, near),
            (4, crossing),
            (5, by_way),
        ):
            if kind < 4 or detour:
                pl.when(there)(functools.partial(kv_copy(group, kind).wait_send))


def per_device(
    tokens,
    norm_gain,
    w_query,
    w_key,
    w_value,
    query_gain,
    key_gain,
    w_out,
    block_lists,
    block_counts,
):
    rows, depth = tokens.shape
    width = w_query.shape[1]
    dma = pltpu.SemaphoreType.DMA
    bf16 = jnp.bfloat16
    hbm = pl.BlockSpec(memory_space=pltpu.HBM)
    terms = pl.pallas_call(
        functools.partial(kernel, lax.axis_size("frame")),
        out_shape=[jax.ShapeDtypeStruct((rows, depth), bf16)] * 3,
        in_specs=[hbm] * 10,
        out_specs=[hbm] * 3,
        scratch_shapes=[
            pltpu.VMEM((rows, depth), bf16),
            pltpu.VMEM((1, depth), jnp.float32),
            pltpu.VMEM((1, HD), jnp.float32),
            pltpu.VMEM((1, HD), jnp.float32),
            pltpu.SMEM(block_lists.shape, jnp.int32),
            pltpu.SMEM(block_counts.shape, jnp.int32),
            pltpu.VMEM((depth, width), bf16),
            pltpu.VMEM((depth, width), bf16),
            pltpu.VMEM((depth, width), bf16),
            pltpu.VMEM((2 * width, depth), bf16),
            pltpu.VMEM((8, rows, depth), bf16),
            pltpu.VMEM((8, rows, width), bf16),
            pltpu.VMEM(((2 * BAND + 1) * 8, rows, 2 * width), bf16),
            pltpu.VMEM((4, 3, rows, width), bf16),
            pltpu.VMEM((4, rows, depth), bf16),
            pltpu.VMEM((rows, depth), bf16),
            dma((10,)),
            dma((7 * PIECES,)),
            dma((7 * PIECES,)),
            dma((24,)),
            dma((24,)),
            dma((2,)),
            dma((2,)),
            dma((4,)),
            dma((4,)),
            dma((3 * PIECES,)),
            dma((3 * PIECES,)),
        ],
        compiler_params=pltpu.CompilerParams(
            collective_id=0, has_side_effects=True, vmem_limit_bytes=63 * 1024 * 1024
        ),
    )(
        tokens,
        norm_gain.reshape(1, depth),
        query_gain.reshape(1, HD),
        key_gain.reshape(1, HD),
        block_lists,
        block_counts,
        w_query,
        w_key,
        w_value,
        w_out,
    )
    own, from_right, from_left = (term.astype(jnp.float32) for term in terms)
    return (own + from_right + from_left).astype(bf16)


def solution(mesh):
    placed = (
        P(("frame", "head"), None),
        P(),
        P(None, "head"),
        P(None, "head"),
        P(None, "head"),
        P(),
        P(),
        P("head", None),
        P("frame", None),
        P("frame"),
    )
    return jax.shard_map(
        per_device,
        mesh=mesh,
        in_specs=placed,
        out_specs=P(("frame", "head"), None),
        check_vma=False,
    )
```

```python
import functools

import jax
import jax.numpy as jnp
from jax import lax
from jax.experimental import pallas as pl
from jax.experimental.pallas import tpu as pltpu
from jax.sharding import PartitionSpec as P

HD = 128
BLK = 128
MAXB = 6
BAND = 2
NB = 4
EPS = 1e-06
PIECES = 4
BY_WAY_UP = 0
BY_WAY_DOWN = 2
BY_WAY = max(BY_WAY_UP, BY_WAY_DOWN)
MESH = pl.DeviceIdType.MESH

SLOT = (0, 2, 1, 3)


def kernel(
    frames,
    tokens_hbm,
    ngain_hbm,
    qgain_hbm,
    kgain_hbm,
    lists_hbm,
    counts_hbm,
    wq_hbm,
    wk_hbm,
    wv_hbm,
    wo_hbm,
    own_hbm,
    from_right_hbm,
    from_left_hbm,
    tokens_ref,
    ngain_ref,
    qgain_ref,
    kgain_ref,
    lists_ref,
    counts_ref,
    wq,
    wk,
    wv,
    wo,
    xn,
    q,
    kv,
    ctx,
    part,
    got_h,
    in_sem,
    ag_s,
    ag_r,
    kv_s,
    kv_r,
    wo_s,
    wo_r,
    ctx_s,
    ctx_r,
    rs_s,
    rs_r,
):
    f = lax.axis_index("frame")
    head = lax.axis_index("head")
    x, y = head // 2, head % 2
    core = f % 2
    toward = 1 - 2 * core
    right, left = (x + 1) % 4, (x + 3) % 4
    to_right, to_left = {"head": right * 2 + y}, {"head": left * 2 + y}
    to_other = {"head": x * 2 + 1 - y}
    to_sibling = {"frame": f + toward}
    to_far = {"frame": f + 2 * toward}
    to_near = {"frame": f - toward}
    to_across = {"frame": (f + frames // 2) % frames, "head": x * 2 + 1 - y}
    rows = tokens_ref.shape[0]
    half, piece = rows // 2, rows // PIECES
    width = wq.shape[1]
    heads = width // HD

    def within(d):
        return jnp.logical_and(f + d >= 0, f + d < frames)

    far_to, far_from, near = within(2 * toward), within(-2 * toward), within(-toward)
    mid = frames // 2
    crossing = jnp.logical_or(
        jnp.logical_and(f == mid - 1, core == 1), jnp.logical_and(f == mid, core == 0)
    )
    close = jnp.logical_and(near, jnp.logical_not(crossing))
    spare = jnp.logical_or(f < 2, f >= frames - 2)
    usual = jnp.logical_not(spare)
    by_way = jnp.logical_not(far_to)

    def in_use(group, there, upper):
        up = jnp.logical_and(upper == 1, group < BY_WAY_UP)
        down = jnp.logical_and(upper == 0, group < BY_WAY_DOWN)
        return jnp.logical_and(there, jnp.logical_or(up, down))

    def cross_by_way(group):
        return in_use(group, crossing, 1 - f // mid)

    def passes(group):
        return in_use(group, by_way, f // mid)

    def near_directly(group):
        return jnp.logical_and(near, jnp.logical_not(cross_by_way(group)))

    to_way = {"frame": f - toward * (mid - 1)}
    from_way = {"frame": f + toward * (mid - 2)}
    to_crossing = {"frame": f - toward * (mid - 2)}

    loads = [
        pltpu.make_async_copy(src, dst, in_sem.at[i])
        for i, (src, dst) in enumerate(
            (
                (tokens_hbm, tokens_ref),
                (ngain_hbm, ngain_ref),
                (qgain_hbm, qgain_ref),
                (kgain_hbm, kgain_ref),
                (lists_hbm, lists_ref),
                (counts_hbm, counts_ref),
                (wk_hbm, wk),
                (wv_hbm, wv),
                (wq_hbm, wq),
                (wo_hbm, wo.at[0:width]),
            )
        )
    ]
    loads[0].start()
    loads[1].start()

    barrier = pltpu.get_barrier_semaphore()

    def greet(device):
        pl.semaphore_signal(barrier, inc=1, device_id=device, device_id_type=MESH)

    for device in (to_right, to_left, to_other, to_sibling, to_across):
        greet(device)
    peers = 5
    for there, device in (
        (far_to, to_far),
        (far_from, {"frame": f - 2 * toward}),
        (near, to_near),
        (crossing, to_way),
        (crossing, from_way),
        (by_way, to_way),
        (by_way, to_crossing),
    ):
        pl.when(there)(functools.partial(greet, device))
        peers = peers + jnp.where(there, 1, 0)

    loads[0].wait()
    loads[1].wait()
    for copy in loads[2:]:
        copy.start()
    wide = tokens_ref[...].astype(jnp.float32)
    factor = lax.rsqrt(jnp.mean(wide * wide, axis=-1, keepdims=True) + EPS)
    xn[0] = (wide * factor * ngain_ref[...]).astype(jnp.bfloat16)

    pl.semaphore_wait(barrier, peers)

    sent = []

    def send(src, dst, sems, index, device, keep=True):
        copy = pltpu.make_async_remote_copy(
            src_ref=src,
            dst_ref=dst,
            send_sem=sems[0].at[index],
            recv_sem=sems[1].at[index],
            device_id=device,
            device_id_type=MESH,
        )
        if keep:
            sent.append(copy)
        return copy

    def rows_of(p):
        return pl.ds(p * piece, piece)

    ag = (ag_s, ag_r)
    a_right, a_left, b_other, f_ward, c_right, c_left, d_other = [], [], [], [], [], [], []
    c_full, e_other = [], []
    depth = xn.shape[2]
    cut = depth * 2 // 3
    most, rest, every = pl.ds(0, cut), pl.ds(cut, depth - cut), pl.ds(0, depth)
    for p in range(PIECES):
        r = rows_of(p)
        n = 8 * p
        a_right.append(send(xn.at[0, r], xn.at[3, r], ag, n, to_right))
        a_left.append(send(xn.at[0, r], xn.at[2, r], ag, n + 1, to_left))
        b_other.append(send(xn.at[0, r], xn.at[4, r], ag, n + 2, to_other))
        if p % 2:
            f_ward.append(send(xn.at[3, r], xn.at[1, r], ag, n + 3, to_right))
        else:
            f_ward.append(send(xn.at[2, r], xn.at[1, r], ag, n + 3, to_left))
        right_columns, left_columns = (most, every) if p % 2 else (every, most)
        c_right.append(
            send(xn.at[4, r, right_columns], xn.at[7, r, right_columns], ag, n + 4, to_right, False)
        )
        c_left.append(
            send(xn.at[4, r, left_columns], xn.at[6, r, left_columns], ag, n + 5, to_left, False)
        )
        if p % 2:
            c_full.append(send(xn.at[4, r], xn.at[7, r], ag, n + 4, to_right, False))
            e_other.append(send(xn.at[3, r, rest], xn.at[7, r, rest], ag, n + 7, to_other, False))
        else:
            c_full.append(send(xn.at[4, r], xn.at[6, r], ag, n + 5, to_left, False))
            e_other.append(send(xn.at[2, r, rest], xn.at[6, r, rest], ag, n + 7, to_other, False))
        d_other.append(send(xn.at[1, r], xn.at[5, r], ag, n + 6, to_other, False))
    g_right = send(xn.at[7, rows_of(2)], xn.at[5, rows_of(2)], ag, 22, to_right, False)
    g_left = send(xn.at[6, rows_of(3)], xn.at[5, rows_of(3)], ag, 30, to_left, False)

    def thrice(p, what):
        (getattr(c_left[p], what) if p % 2 else getattr(c_right[p], what))()
        cut_one = c_right[p] if p % 2 else c_left[p]

        @pl.when(usual)
        def _():
            getattr(cut_one, what)()
            if what != "start":
                getattr(e_other[p], what)()

        @pl.when(spare)
        def _():
            getattr(c_full[p], what)()

    def normed_heads(section, gain_ref):
        done = []
        for i in range(heads):
            part_i = section[:, i * HD : (i + 1) * HD]
            scale = lax.rsqrt(jnp.mean(part_i * part_i, axis=-1, keepdims=True) + EPS)
            done.append((part_i * scale * gain_ref[...]).astype(jnp.bfloat16))
        return done

    groups = (
        (0, 1, 0, rows),
        (2, 3, 0, rows),
        (1, 1, 0, rows),
        (5, 3, 0, half),
        (5, 3, half, piece),
        (5, 3, half + piece, piece),
    )

    def gathered(group):
        slot, count, low, each = groups[group]
        block = xn[slot : slot + count, low : low + each]
        return block.reshape(count * each, block.shape[-1])

    def kv_copy(group, kind):
        slot, count, low, each = groups[group]
        out, into, device, send_kind, recv_kind = (
            (BAND, BAND - toward, to_sibling, 0, 0),
            (BAND, BAND - 2 * toward, to_far, 1, 1),
            (BAND, BAND + toward, to_near, 2, 2),
            (BAND - toward, BAND - 2 * toward, to_sibling, 3, 3),
            (BAND, BAND - 2 * toward, to_way, 2, 3),
            (BAND + 2 * toward, BAND - toward, to_crossing, 1, 2),
        )[kind]
        r = pl.ds(low, each)
        return pltpu.make_async_remote_copy(
            src_ref=kv.at[pl.ds(out * 8 + slot, count), r],
            dst_ref=kv.at[pl.ds(into * 8 + slot, count), r],
            send_sem=kv_s.at[send_kind * len(groups) + group],
            recv_sem=kv_r.at[recv_kind * len(groups) + group],
            device_id=device,
            device_id_type=MESH,
        )

    def project_pairs(group):
        slot, count, low, each = groups[group]
        block = gathered(group)
        keys = jnp.dot(block, wk[...], preferred_element_type=jnp.float32)
        pieces = normed_heads(keys, kgain_ref)
        values = jnp.dot(block, wv[...], preferred_element_type=jnp.float32).astype(jnp.bfloat16)
        for n in range(count):
            at, r = BAND * 8 + slot + n, slice(n * each, (n + 1) * each)
            for i in range(heads):
                kv[at, low : low + each, i * HD : (i + 1) * HD] = pieces[i][r]
            kv[at, low : low + each, width:] = values[r]
        if group < BY_WAY:
            pl.when(near_directly(group))(lambda: kv_copy(group, 2).start())
            pl.when(cross_by_way(group))(lambda: kv_copy(group, 4).start())
        else:
            pl.when(near)(lambda: kv_copy(group, 2).start())
        pl.when(far_to)(lambda: kv_copy(group, 1).start())
        kv_copy(group, 0).start()

    def project_queries(group):
        slot, count, low, each = groups[group]
        queries = jnp.dot(gathered(group), wq[...], preferred_element_type=jnp.float32)
        pieces = normed_heads(queries, qgain_ref)
        for n in range(count):
            for i in range(heads):
                q[slot + n, low : low + each, i * HD : (i + 1) * HD] = pieces[i][
                    n * each : (n + 1) * each
                ]

    def pass_on(group):
        @pl.when(passes(group))
        def _():
            kv_copy(group, 3).wait_recv()
            kv_copy(group, 5).start()

    def relay(group, there):
        @pl.when(there)
        def _():
            kv_copy(group, 2).wait_recv()
            kv_copy(group, 3).start()

    for p in range(PIECES):
        a_right[(1, 3, 0, 2)[p]].start()
        a_left[p if p in (0, 3) else 3 - p].start()
        b_other[p].start()

    share = width // 2
    wo_send = send(
        wo_hbm.at[pl.ds(core * share, share)],
        wo.at[pl.ds(width + core * share, share)],
        (wo_s, wo_r),
        0,
        to_across,
    )
    wo_pass = send(
        wo.at[pl.ds(width + core * share, share)],
        wo.at[pl.ds(width + core * share, share)],
        (wo_s, wo_r),
        1,
        to_sibling,
    )
    wo_send.start()

    for copy in loads[2:8]:
        copy.wait()
    project_pairs(0)
    loads[8].wait()
    project_queries(0)

    for early, late in ((0, 1), (2, 3)):
        a_right[late].wait_recv()
        f_ward[late].start()
        pl.when(usual)(e_other[late].start)
        a_left[early].wait_recv()
        f_ward[early].start()
        pl.when(usual)(e_other[early].start)
    for p in range(PIECES):
        b_other[p].wait_recv()
        thrice(p, "start")
    for p in (0, 2):
        a_right[p].wait_recv()
        a_left[p + 1].wait_recv()
    project_pairs(1)
    for p in range(PIECES):
        f_ward[p].wait_recv()
        if p < 2:
            d_other[p].start()
        else:
            pl.when(usual)(d_other[p].start)
    pass_on(0)
    project_queries(1)
    project_pairs(2)
    project_queries(2)
    relay(0, close)
    for first, last, group in ((0, 2, 3), (2, 3, 4), (3, 4, 5)):
        for p in range(first, last):
            if group < 5:
                thrice(p, "wait_recv")
            if group == 4:
                thrice(3, "wait_recv")
                pl.when(spare)(g_right.start)
                pl.when(spare)(g_left.start)
            d_other[p].wait_recv()
        project_pairs(group)
        if group - 2 < BY_WAY:
            pass_on(group - 2)
        if group < 5:
            project_queries(group)
        relay(group - 2, close)
    project_queries(5)
    loads[9].wait()
    wo_send.wait_recv()
    wo_pass.start()
    relay(4, close)
    relay(5, close)
    for group in range(len(groups)):
        relay(group, crossing)

    for group in range(len(groups)):
        kv_copy(group, 0).wait_recv()

        @pl.when(far_from)
        def _():
            kv_copy(group, 1).wait_recv()

        @pl.when(far_to)
        def _():
            kv_copy(group, 3).wait_recv()

    score_factor = 1.0 / HD**0.5

    def attend(k):
        block = (x + k) % 4
        own = SLOT[k]
        queries = jnp.concatenate([q[own], q[own + 4]], axis=0)
        listed = counts_ref[block]
        pairs, on = [], []
        for m in range(MAXB):
            live = m < listed
            picked = jnp.where(live, lists_ref[block, m], f * NB + block)
            frame = jnp.clip(picked // NB - f + BAND, 0, 2 * BAND)
            across = (picked % NB - x + 4) % 4
            spot = frame * 8 + (across % 2) * 2 + across // 2
            pairs += [kv[spot], kv[spot + 4]]
            on.append(jnp.where(live, 1.0, 0.0).astype(jnp.float32))
        weighted, totals = [], []
        for i in range(heads):
            keys = jnp.concatenate([pair[:, i * HD : (i + 1) * HD] for pair in pairs], axis=0)
            values = jnp.concatenate(
                [pair[:, width + i * HD : width + (i + 1) * HD] for pair in pairs], axis=0
            )
            scores = lax.dot_general(
                queries[:, i * HD : (i + 1) * HD],
                keys,
                (((1,), (1,)), ((), ())),
                preferred_element_type=jnp.float32,
            )
            weights = [
                jnp.exp(scores[:, m * BLK : (m + 1) * BLK] * score_factor) * on[m]
                for m in range(MAXB)
            ]
            summed = functools.reduce(jnp.add, weights)
            totals.append(jnp.sum(summed, axis=-1, keepdims=True))
            rounded = jnp.concatenate([weight.astype(jnp.bfloat16) for weight in weights], axis=1)
            weighted.append(jnp.dot(rounded, values, preferred_element_type=jnp.float32))
        for i in range(heads):
            done = (weighted[i] / totals[i]).astype(jnp.bfloat16)
            ctx[k, 0, :, i * HD : (i + 1) * HD] = done[0:rows]
            ctx[k, 1, :, i * HD : (i + 1) * HD] = done[rows:]

    ctx_sends = [
        send(ctx.at[k, 1], ctx.at[k, 2], (ctx_s, ctx_r), k, to_other) for k in range(4)
    ]

    def out_project(k):
        partial = jnp.dot(ctx[k, 0], wo[0:width], preferred_element_type=jnp.float32)
        partial = partial + jnp.dot(ctx[k, 2], wo[width:], preferred_element_type=jnp.float32)
        part[k] = partial.astype(jnp.bfloat16)

    rs = (rs_s, rs_r)
    h_left, h_right, c_l, c_r = [], [], [], []
    for p in range(PIECES):
        r = rows_of(p)
        if p < PIECES // 2:
            h_left.append(send(part.at[2, r], got_h.at[r], rs, 3 * p, to_left))
        else:
            h_right.append(send(part.at[2, r], got_h.at[r], rs, 3 * p, to_right))
        c_l.append(send(part.at[3, r], from_right_hbm.at[r], rs, 3 * p + 1, to_left))
        c_r.append(send(part.at[1, r], from_left_hbm.at[r], rs, 3 * p + 2, to_right))

    for k in (2, 3, 1):
        attend(k)
        ctx_sends[k].start()
    wo_pass.wait_recv()
    ctx_sends[2].wait_recv()
    out_project(2)
    for p in range(2):
        h_left[p].start()
        h_right[p].start()
    attend(0)
    ctx_sends[0].start()
    ctx_sends[3].wait_recv()
    out_project(3)
    c_l[2].start()
    c_l[3].start()
    ctx_sends[1].wait_recv()
    out_project(1)
    c_r[0].start()
    c_r[1].start()

    def add_in(k, p):
        r = slice(p * piece, (p + 1) * piece)
        total = part[k, r].astype(jnp.float32) + got_h[r].astype(jnp.float32)
        part[k, r] = total.astype(jnp.bfloat16)

    for p in range(2):
        h_left[p].wait_recv()
        add_in(3, p)
        c_l[p].start()
        h_right[p].wait_recv()
        add_in(1, p + 2)
        c_r[p + 2].start()
    ctx_sends[0].wait_recv()
    out_project(0)
    mine = pltpu.make_async_copy(part.at[0], own_hbm, in_sem.at[0])
    mine.start()
    for p in (2, 3, 0, 1):
        c_l[p].wait_recv()
        c_r[(p + 2) % 4].wait_recv()
    mine.wait()

    for copy in sent + d_other:
        copy.wait_send()
    for p in range(PIECES):
        thrice(p, "wait_send")
    for group in range(len(groups)):
        kv_copy(group, 0).wait_send()
        ends = ((1, far_to), (2, near), (3, near))
        if group < BY_WAY:
            ends = ((1, far_to), (2, near_directly(group)), (3, near))
            ends += ((4, cross_by_way(group)), (5, passes(group)))
        for kind, there in ends:
            pl.when(there)(kv_copy(group, kind).wait_send)


def per_device(
    tokens,
    norm_gain,
    w_query,
    w_key,
    w_value,
    query_gain,
    key_gain,
    w_out,
    block_lists,
    block_counts,
):
    rows, depth = tokens.shape
    width = w_query.shape[1]
    dma = pltpu.SemaphoreType.DMA
    bf16 = jnp.bfloat16
    hbm = pl.BlockSpec(memory_space=pltpu.HBM)
    terms = pl.pallas_call(
        functools.partial(kernel, lax.axis_size("frame")),
        out_shape=[jax.ShapeDtypeStruct((rows, depth), bf16)] * 3,
        in_specs=[hbm] * 10,
        out_specs=[hbm] * 3,
        scratch_shapes=[
            pltpu.VMEM((rows, depth), bf16),
            pltpu.VMEM((1, depth), jnp.float32),
            pltpu.VMEM((1, HD), jnp.float32),
            pltpu.VMEM((1, HD), jnp.float32),
            pltpu.SMEM(block_lists.shape, jnp.int32),
            pltpu.SMEM(block_counts.shape, jnp.int32),
            pltpu.VMEM((depth, width), bf16),
            pltpu.VMEM((depth, width), bf16),
            pltpu.VMEM((depth, width), bf16),
            pltpu.VMEM((2 * width, depth), bf16),
            pltpu.VMEM((8, rows, depth), bf16),
            pltpu.VMEM((8, rows, width), bf16),
            pltpu.VMEM(((2 * BAND + 1) * 8, rows, 2 * width), bf16),
            pltpu.VMEM((4, 3, rows, width), bf16),
            pltpu.VMEM((4, rows, depth), bf16),
            pltpu.VMEM((rows, depth), bf16),
            dma((10,)),
            dma((8 * PIECES,)),
            dma((8 * PIECES,)),
            dma((24,)),
            dma((24,)),
            dma((2,)),
            dma((2,)),
            dma((4,)),
            dma((4,)),
            dma((3 * PIECES,)),
            dma((3 * PIECES,)),
        ],
        compiler_params=pltpu.CompilerParams(
            collective_id=0, has_side_effects=True, vmem_limit_bytes=63 * 1024 * 1024
        ),
    )(
        tokens,
        norm_gain.reshape(1, depth),
        query_gain.reshape(1, HD),
        key_gain.reshape(1, HD),
        block_lists,
        block_counts,
        w_query,
        w_key,
        w_value,
        w_out,
    )
    own, from_right, from_left = (term.astype(jnp.float32) for term in terms)
    return (own + from_right + from_left).astype(bf16)


def solution(mesh):
    placed = (
        P(("frame", "head"), None),
        P(),
        P(None, "head"),
        P(None, "head"),
        P(None, "head"),
        P(),
        P(),
        P("head", None),
        P("frame", None),
        P("frame"),
    )
    return jax.shard_map(
        per_device,
        mesh=mesh,
        in_specs=placed,
        out_specs=P(("frame", "head"), None),
        check_vma=False,
    )
```

```python
import functools

import jax
import jax.numpy as jnp
from jax import lax
from jax.experimental import pallas as pl
from jax.experimental.pallas import tpu as pltpu
from jax.sharding import PartitionSpec as P

HD = 128
BLK = 128
MAXB = 6
BAND = 2
NB = 4
EPS = 1e-06
PIECES = 4
BY_WAY_UP = 0
BY_WAY_DOWN = 2
BY_WAY = max(BY_WAY_UP, BY_WAY_DOWN)
MESH = pl.DeviceIdType.MESH

SLOT = (0, 2, 1, 3)


def kernel(
    frames,
    tokens_hbm,
    ngain_hbm,
    qgain_hbm,
    kgain_hbm,
    lists_hbm,
    counts_hbm,
    wq_hbm,
    wk_hbm,
    wv_hbm,
    wo_hbm,
    own_hbm,
    from_right_hbm,
    from_left_hbm,
    tokens_ref,
    ngain_ref,
    qgain_ref,
    kgain_ref,
    lists_ref,
    counts_ref,
    wq,
    wk,
    wv,
    wo,
    xn,
    q,
    kv,
    ctx,
    part,
    got_h,
    in_sem,
    ag_s,
    ag_r,
    kv_s,
    kv_r,
    wo_s,
    wo_r,
    ctx_s,
    ctx_r,
    rs_s,
    rs_r,
):
    f = lax.axis_index("frame")
    head = lax.axis_index("head")
    x, y = head // 2, head % 2
    core = f % 2
    toward = 1 - 2 * core
    right, left = (x + 1) % 4, (x + 3) % 4
    to_right, to_left = {"head": right * 2 + y}, {"head": left * 2 + y}
    to_other = {"head": x * 2 + 1 - y}
    to_sibling = {"frame": f + toward}
    to_far = {"frame": f + 2 * toward}
    to_near = {"frame": f - toward}
    to_across = {"frame": (f + frames // 2) % frames, "head": x * 2 + 1 - y}
    rows = tokens_ref.shape[0]
    half, piece = rows // 2, rows // PIECES
    width = wq.shape[1]
    heads = width // HD

    def within(d):
        return jnp.logical_and(f + d >= 0, f + d < frames)

    far_to, far_from, near = within(2 * toward), within(-2 * toward), within(-toward)
    mid = frames // 2
    crossing = jnp.logical_or(
        jnp.logical_and(f == mid - 1, core == 1), jnp.logical_and(f == mid, core == 0)
    )
    close = jnp.logical_and(near, jnp.logical_not(crossing))
    spare = jnp.logical_or(f < 2, f >= frames - 2)
    usual = jnp.logical_not(spare)
    spare_all = f < 2
    spare_half = jnp.logical_and(spare, f >= 2)
    by_way = jnp.logical_not(far_to)

    def in_use(group, there, upper):
        up = jnp.logical_and(upper == 1, group < BY_WAY_UP)
        down = jnp.logical_and(upper == 0, group < BY_WAY_DOWN)
        return jnp.logical_and(there, jnp.logical_or(up, down))

    def cross_by_way(group):
        return in_use(group, crossing, 1 - f // mid)

    def passes(group):
        return in_use(group, by_way, f // mid)

    def near_directly(group):
        return jnp.logical_and(near, jnp.logical_not(cross_by_way(group)))

    to_way = {"frame": f - toward * (mid - 1)}
    from_way = {"frame": f + toward * (mid - 2)}
    to_crossing = {"frame": f - toward * (mid - 2)}

    loads = [
        pltpu.make_async_copy(src, dst, in_sem.at[i])
        for i, (src, dst) in enumerate(
            (
                (tokens_hbm, tokens_ref),
                (ngain_hbm, ngain_ref),
                (qgain_hbm, qgain_ref),
                (kgain_hbm, kgain_ref),
                (lists_hbm, lists_ref),
                (counts_hbm, counts_ref),
                (wk_hbm, wk),
                (wv_hbm, wv),
                (wq_hbm, wq),
                (wo_hbm, wo.at[0:width]),
            )
        )
    ]
    loads[0].start()
    loads[1].start()

    barrier = pltpu.get_barrier_semaphore()

    def greet(device):
        pl.semaphore_signal(barrier, inc=1, device_id=device, device_id_type=MESH)

    for device in (to_right, to_left, to_other, to_sibling, to_across):
        greet(device)
    peers = 5
    for there, device in (
        (far_to, to_far),
        (far_from, {"frame": f - 2 * toward}),
        (near, to_near),
        (crossing, to_way),
        (crossing, from_way),
        (by_way, to_way),
        (by_way, to_crossing),
    ):
        pl.when(there)(functools.partial(greet, device))
        peers = peers + jnp.where(there, 1, 0)

    loads[0].wait()
    loads[1].wait()
    for copy in loads[2:]:
        copy.start()
    wide = tokens_ref[...].astype(jnp.float32)
    factor = lax.rsqrt(jnp.mean(wide * wide, axis=-1, keepdims=True) + EPS)
    xn[0] = (wide * factor * ngain_ref[...]).astype(jnp.bfloat16)

    pl.semaphore_wait(barrier, peers)

    sent = []

    def send(src, dst, sems, index, device, keep=True):
        copy = pltpu.make_async_remote_copy(
            src_ref=src,
            dst_ref=dst,
            send_sem=sems[0].at[index],
            recv_sem=sems[1].at[index],
            device_id=device,
            device_id_type=MESH,
        )
        if keep:
            sent.append(copy)
        return copy

    def rows_of(p):
        return pl.ds(p * piece, piece)

    ag = (ag_s, ag_r)
    a_right, a_left, b_other, f_ward, c_right, c_left, d_other = [], [], [], [], [], [], []
    c_full, e_other = [], []
    depth = xn.shape[2]
    cut = depth * 2 // 3
    most, rest, every = pl.ds(0, cut), pl.ds(cut, depth - cut), pl.ds(0, depth)
    for p in range(PIECES):
        r = rows_of(p)
        n = 8 * p
        a_right.append(send(xn.at[0, r], xn.at[3, r], ag, n, to_right))
        a_left.append(send(xn.at[0, r], xn.at[2, r], ag, n + 1, to_left))
        b_other.append(send(xn.at[0, r], xn.at[4, r], ag, n + 2, to_other))
        if p % 2:
            f_ward.append(send(xn.at[3, r], xn.at[1, r], ag, n + 3, to_right))
        else:
            f_ward.append(send(xn.at[2, r], xn.at[1, r], ag, n + 3, to_left))
        right_columns, left_columns = (most, every) if p % 2 else (every, most)
        c_right.append(
            send(xn.at[4, r, right_columns], xn.at[7, r, right_columns], ag, n + 4, to_right, False)
        )
        c_left.append(
            send(xn.at[4, r, left_columns], xn.at[6, r, left_columns], ag, n + 5, to_left, False)
        )
        if p % 2:
            c_full.append(send(xn.at[4, r], xn.at[7, r], ag, n + 4, to_right, False))
            e_other.append(send(xn.at[3, r, rest], xn.at[7, r, rest], ag, n + 7, to_other, False))
        else:
            c_full.append(send(xn.at[4, r], xn.at[6, r], ag, n + 5, to_left, False))
            e_other.append(send(xn.at[2, r, rest], xn.at[6, r, rest], ag, n + 7, to_other, False))
        d_other.append(send(xn.at[1, r], xn.at[5, r], ag, n + 6, to_other, False))
    g_right = send(xn.at[7, rows_of(2)], xn.at[5, rows_of(2)], ag, 22, to_right, False)
    g_left = send(xn.at[6, rows_of(3)], xn.at[5, rows_of(3)], ag, 30, to_left, False)
    g_first = send(xn.at[7, rows_of(0)], xn.at[5, rows_of(0)], ag, 6, to_right, False)
    g_second = send(xn.at[6, rows_of(1)], xn.at[5, rows_of(1)], ag, 14, to_left, False)

    def thrice(p, what):
        (getattr(c_left[p], what) if p % 2 else getattr(c_right[p], what))()
        cut_one = c_right[p] if p % 2 else c_left[p]

        @pl.when(usual)
        def _():
            getattr(cut_one, what)()
            if what != "start":
                getattr(e_other[p], what)()

        @pl.when(spare)
        def _():
            getattr(c_full[p], what)()

    def normed_heads(section, gain_ref):
        done = []
        for i in range(heads):
            part_i = section[:, i * HD : (i + 1) * HD]
            scale = lax.rsqrt(jnp.mean(part_i * part_i, axis=-1, keepdims=True) + EPS)
            done.append((part_i * scale * gain_ref[...]).astype(jnp.bfloat16))
        return done

    groups = (
        (0, 1, 0, rows),
        (2, 3, 0, rows),
        (1, 1, 0, rows),
        (5, 3, 0, half),
        (5, 3, half, piece),
        (5, 3, half + piece, piece),
    )

    def gathered(group):
        slot, count, low, each = groups[group]
        block = xn[slot : slot + count, low : low + each]
        return block.reshape(count * each, block.shape[-1])

    def kv_copy(group, kind):
        slot, count, low, each = groups[group]
        out, into, device, send_kind, recv_kind = (
            (BAND, BAND - toward, to_sibling, 0, 0),
            (BAND, BAND - 2 * toward, to_far, 1, 1),
            (BAND, BAND + toward, to_near, 2, 2),
            (BAND - toward, BAND - 2 * toward, to_sibling, 3, 3),
            (BAND, BAND - 2 * toward, to_way, 2, 3),
            (BAND + 2 * toward, BAND - toward, to_crossing, 1, 2),
        )[kind]
        r = pl.ds(low, each)
        return pltpu.make_async_remote_copy(
            src_ref=kv.at[pl.ds(out * 8 + slot, count), r],
            dst_ref=kv.at[pl.ds(into * 8 + slot, count), r],
            send_sem=kv_s.at[send_kind * len(groups) + group],
            recv_sem=kv_r.at[recv_kind * len(groups) + group],
            device_id=device,
            device_id_type=MESH,
        )

    def project_pairs(group):
        slot, count, low, each = groups[group]
        block = gathered(group)
        keys = jnp.dot(block, wk[...], preferred_element_type=jnp.float32)
        pieces = normed_heads(keys, kgain_ref)
        values = jnp.dot(block, wv[...], preferred_element_type=jnp.float32).astype(jnp.bfloat16)
        for n in range(count):
            at, r = BAND * 8 + slot + n, slice(n * each, (n + 1) * each)
            for i in range(heads):
                kv[at, low : low + each, i * HD : (i + 1) * HD] = pieces[i][r]
            kv[at, low : low + each, width:] = values[r]
        if group < BY_WAY:
            pl.when(near_directly(group))(lambda: kv_copy(group, 2).start())
            pl.when(cross_by_way(group))(lambda: kv_copy(group, 4).start())
        else:
            pl.when(near)(lambda: kv_copy(group, 2).start())
        pl.when(far_to)(lambda: kv_copy(group, 1).start())
        kv_copy(group, 0).start()

    def project_queries(group):
        slot, count, low, each = groups[group]
        queries = jnp.dot(gathered(group), wq[...], preferred_element_type=jnp.float32)
        pieces = normed_heads(queries, qgain_ref)
        for n in range(count):
            for i in range(heads):
                q[slot + n, low : low + each, i * HD : (i + 1) * HD] = pieces[i][
                    n * each : (n + 1) * each
                ]

    def pass_on(group):
        @pl.when(passes(group))
        def _():
            kv_copy(group, 3).wait_recv()
            kv_copy(group, 5).start()

    def relay(group, there):
        @pl.when(there)
        def _():
            kv_copy(group, 2).wait_recv()
            kv_copy(group, 3).start()

    for p in range(PIECES):
        a_right[(1, 3, 0, 2)[p]].start()
        a_left[p if p in (0, 3) else 3 - p].start()
        b_other[p].start()

    share = width // 2
    wo_send = send(
        wo_hbm.at[pl.ds(core * share, share)],
        wo.at[pl.ds(width + core * share, share)],
        (wo_s, wo_r),
        0,
        to_across,
    )
    wo_pass = send(
        wo.at[pl.ds(width + core * share, share)],
        wo.at[pl.ds(width + core * share, share)],
        (wo_s, wo_r),
        1,
        to_sibling,
    )
    wo_send.start()

    for copy in loads[2:8]:
        copy.wait()
    project_pairs(0)
    loads[8].wait()
    project_queries(0)

    for early, late in ((0, 1), (2, 3)):
        a_right[late].wait_recv()
        f_ward[late].start()
        pl.when(usual)(e_other[late].start)
        a_left[early].wait_recv()
        f_ward[early].start()
        pl.when(usual)(e_other[early].start)
    for p in range(PIECES):
        b_other[p].wait_recv()
        thrice(p, "start")
    for p in (0, 2):
        a_right[p].wait_recv()
        a_left[p + 1].wait_recv()
    project_pairs(1)
    for p in range(PIECES):
        f_ward[p].wait_recv()
        pl.when(f >= 2 if p < 2 else usual)(d_other[p].start)
    pass_on(0)
    project_queries(1)
    project_pairs(2)
    project_queries(2)
    relay(0, close)
    for first, last, group in ((0, 2, 3), (2, 3, 4), (3, 4, 5)):
        for p in range(first, last):
            if group == 3:
                thrice(p, "wait_recv")
        if group == 3:

            @pl.when(spare_all)
            def _():
                g_first.start()
                g_second.start()
                thrice(2, "wait_recv")
                g_right.start()
                thrice(3, "wait_recv")
                g_left.start()

        if group == 4:

            @pl.when(f >= 2)
            def _():
                thrice(2, "wait_recv")
                pl.when(spare_half)(g_right.start)
                thrice(3, "wait_recv")
                pl.when(spare_half)(g_left.start)

        for p in range(first, last):
            d_other[p].wait_recv()
        project_pairs(group)
        if group - 2 < BY_WAY:
            pass_on(group - 2)
        if group < 5:
            project_queries(group)
        relay(group - 2, close)
    project_queries(5)
    loads[9].wait()
    wo_send.wait_recv()
    wo_pass.start()
    relay(4, close)
    relay(5, close)
    for group in range(len(groups)):
        relay(group, crossing)

    for group in range(len(groups)):
        kv_copy(group, 0).wait_recv()

        @pl.when(far_from)
        def _():
            kv_copy(group, 1).wait_recv()

        @pl.when(far_to)
        def _():
            kv_copy(group, 3).wait_recv()

    score_factor = 1.0 / HD**0.5

    def attend(k):
        block = (x + k) % 4
        own = SLOT[k]
        queries = jnp.concatenate([q[own], q[own + 4]], axis=0)
        listed = counts_ref[block]
        pairs, on = [], []
        for m in range(MAXB):
            live = m < listed
            picked = jnp.where(live, lists_ref[block, m], f * NB + block)
            frame = jnp.clip(picked // NB - f + BAND, 0, 2 * BAND)
            across = (picked % NB - x + 4) % 4
            spot = frame * 8 + (across % 2) * 2 + across // 2
            pairs += [kv[spot], kv[spot + 4]]
            on.append(jnp.where(live, 1.0, 0.0).astype(jnp.float32))
        weighted, totals = [], []
        for i in range(heads):
            keys = jnp.concatenate([pair[:, i * HD : (i + 1) * HD] for pair in pairs], axis=0)
            values = jnp.concatenate(
                [pair[:, width + i * HD : width + (i + 1) * HD] for pair in pairs], axis=0
            )
            scores = lax.dot_general(
                queries[:, i * HD : (i + 1) * HD],
                keys,
                (((1,), (1,)), ((), ())),
                preferred_element_type=jnp.float32,
            )
            weights = [
                jnp.exp(scores[:, m * BLK : (m + 1) * BLK] * score_factor) * on[m]
                for m in range(MAXB)
            ]
            summed = functools.reduce(jnp.add, weights)
            totals.append(jnp.sum(summed, axis=-1, keepdims=True))
            rounded = jnp.concatenate([weight.astype(jnp.bfloat16) for weight in weights], axis=1)
            weighted.append(jnp.dot(rounded, values, preferred_element_type=jnp.float32))
        for i in range(heads):
            done = (weighted[i] / totals[i]).astype(jnp.bfloat16)
            ctx[k, 0, :, i * HD : (i + 1) * HD] = done[0:rows]
            ctx[k, 1, :, i * HD : (i + 1) * HD] = done[rows:]

    ctx_sends = [
        send(ctx.at[k, 1], ctx.at[k, 2], (ctx_s, ctx_r), k, to_other) for k in range(4)
    ]

    def out_project(k):
        partial = jnp.dot(ctx[k, 0], wo[0:width], preferred_element_type=jnp.float32)
        partial = partial + jnp.dot(ctx[k, 2], wo[width:], preferred_element_type=jnp.float32)
        part[k] = partial.astype(jnp.bfloat16)

    rs = (rs_s, rs_r)
    h_left, h_right, c_l, c_r = [], [], [], []
    for p in range(PIECES):
        r = rows_of(p)
        if p < PIECES // 2:
            h_left.append(send(part.at[2, r], got_h.at[r], rs, 3 * p, to_left))
        else:
            h_right.append(send(part.at[2, r], got_h.at[r], rs, 3 * p, to_right))
        c_l.append(send(part.at[3, r], from_right_hbm.at[r], rs, 3 * p + 1, to_left))
        c_r.append(send(part.at[1, r], from_left_hbm.at[r], rs, 3 * p + 2, to_right))

    for k in (2, 3, 1):
        attend(k)
        ctx_sends[k].start()
    wo_pass.wait_recv()
    ctx_sends[2].wait_recv()
    out_project(2)
    for p in range(2):
        h_left[p].start()
        h_right[p].start()
    attend(0)
    ctx_sends[0].start()
    ctx_sends[3].wait_recv()
    out_project(3)
    c_l[2].start()
    c_l[3].start()
    ctx_sends[1].wait_recv()
    out_project(1)
    c_r[0].start()
    c_r[1].start()

    def add_in(k, p):
        r = slice(p * piece, (p + 1) * piece)
        total = part[k, r].astype(jnp.float32) + got_h[r].astype(jnp.float32)
        part[k, r] = total.astype(jnp.bfloat16)

    for p in range(2):
        h_left[p].wait_recv()
        add_in(3, p)
        c_l[p].start()
        h_right[p].wait_recv()
        add_in(1, p + 2)
        c_r[p + 2].start()
    ctx_sends[0].wait_recv()
    out_project(0)
    mine = pltpu.make_async_copy(part.at[0], own_hbm, in_sem.at[0])
    mine.start()
    for p in (2, 3, 0, 1):
        c_l[p].wait_recv()
        c_r[(p + 2) % 4].wait_recv()
    mine.wait()

    for copy in sent + d_other:
        copy.wait_send()
    for p in range(PIECES):
        thrice(p, "wait_send")
    for group in range(len(groups)):
        kv_copy(group, 0).wait_send()
        ends = ((1, far_to), (2, near), (3, near))
        if group < BY_WAY:
            ends = ((1, far_to), (2, near_directly(group)), (3, near))
            ends += ((4, cross_by_way(group)), (5, passes(group)))
        for kind, there in ends:
            pl.when(there)(kv_copy(group, kind).wait_send)


def per_device(
    tokens,
    norm_gain,
    w_query,
    w_key,
    w_value,
    query_gain,
    key_gain,
    w_out,
    block_lists,
    block_counts,
):
    rows, depth = tokens.shape
    width = w_query.shape[1]
    dma = pltpu.SemaphoreType.DMA
    bf16 = jnp.bfloat16
    hbm = pl.BlockSpec(memory_space=pltpu.HBM)
    terms = pl.pallas_call(
        functools.partial(kernel, lax.axis_size("frame")),
        out_shape=[jax.ShapeDtypeStruct((rows, depth), bf16)] * 3,
        in_specs=[hbm] * 10,
        out_specs=[hbm] * 3,
        scratch_shapes=[
            pltpu.VMEM((rows, depth), bf16),
            pltpu.VMEM((1, depth), jnp.float32),
            pltpu.VMEM((1, HD), jnp.float32),
            pltpu.VMEM((1, HD), jnp.float32),
            pltpu.SMEM(block_lists.shape, jnp.int32),
            pltpu.SMEM(block_counts.shape, jnp.int32),
            pltpu.VMEM((depth, width), bf16),
            pltpu.VMEM((depth, width), bf16),
            pltpu.VMEM((depth, width), bf16),
            pltpu.VMEM((2 * width, depth), bf16),
            pltpu.VMEM((8, rows, depth), bf16),
            pltpu.VMEM((8, rows, width), bf16),
            pltpu.VMEM(((2 * BAND + 1) * 8, rows, 2 * width), bf16),
            pltpu.VMEM((4, 3, rows, width), bf16),
            pltpu.VMEM((4, rows, depth), bf16),
            pltpu.VMEM((rows, depth), bf16),
            dma((10,)),
            dma((8 * PIECES,)),
            dma((8 * PIECES,)),
            dma((24,)),
            dma((24,)),
            dma((2,)),
            dma((2,)),
            dma((4,)),
            dma((4,)),
            dma((3 * PIECES,)),
            dma((3 * PIECES,)),
        ],
        compiler_params=pltpu.CompilerParams(
            collective_id=0, has_side_effects=True, vmem_limit_bytes=63 * 1024 * 1024
        ),
    )(
        tokens,
        norm_gain.reshape(1, depth),
        query_gain.reshape(1, HD),
        key_gain.reshape(1, HD),
        block_lists,
        block_counts,
        w_query,
        w_key,
        w_value,
        w_out,
    )
    own, from_right, from_left = (term.astype(jnp.float32) for term in terms)
    return (own + from_right + from_left).astype(bf16)


def solution(mesh):
    placed = (
        P(("frame", "head"), None),
        P(),
        P(None, "head"),
        P(None, "head"),
        P(None, "head"),
        P(),
        P(),
        P("head", None),
        P("frame", None),
        P("frame"),
    )
    return jax.shard_map(
        per_device,
        mesh=mesh,
        in_specs=placed,
        out_specs=P(("frame", "head"), None),
        check_vma=False,
    )
```

```python
import functools

import jax
import jax.numpy as jnp
from jax import lax
from jax.experimental import pallas as pl
from jax.experimental.pallas import tpu as pltpu
from jax.sharding import PartitionSpec as P

HD = 128
BLK = 128
MAXB = 6
BAND = 2
NB = 4
EPS = 1e-06
PIECES = 4
BY_WAY_UP = 0
BY_WAY_DOWN = 2
BY_WAY = max(BY_WAY_UP, BY_WAY_DOWN)
MESH = pl.DeviceIdType.MESH

SLOT = (0, 2, 1, 3)


def kernel(
    frames,
    tokens_hbm,
    ngain_hbm,
    qgain_hbm,
    kgain_hbm,
    lists_hbm,
    counts_hbm,
    wq_hbm,
    wk_hbm,
    wv_hbm,
    wo_hbm,
    own_hbm,
    from_right_hbm,
    from_left_hbm,
    tokens_ref,
    ngain_ref,
    qgain_ref,
    kgain_ref,
    lists_ref,
    counts_ref,
    wq,
    wk,
    wv,
    wo,
    xn,
    q,
    kv,
    ctx,
    part,
    got_h,
    in_sem,
    ag_s,
    ag_r,
    kv_s,
    kv_r,
    wo_s,
    wo_r,
    ctx_s,
    ctx_r,
    rs_s,
    rs_r,
):
    f = lax.axis_index("frame")
    head = lax.axis_index("head")
    x, y = head // 2, head % 2
    core = f % 2
    toward = 1 - 2 * core
    right, left = (x + 1) % 4, (x + 3) % 4
    to_right, to_left = {"head": right * 2 + y}, {"head": left * 2 + y}
    to_other = {"head": x * 2 + 1 - y}
    to_sibling = {"frame": f + toward}
    to_far = {"frame": f + 2 * toward}
    to_near = {"frame": f - toward}
    to_across = {"frame": (f + frames // 2) % frames, "head": x * 2 + 1 - y}
    rows = tokens_ref.shape[0]
    half, piece = rows // 2, rows // PIECES
    width = wq.shape[1]
    heads = width // HD

    def within(d):
        return jnp.logical_and(f + d >= 0, f + d < frames)

    far_to, far_from, near = within(2 * toward), within(-2 * toward), within(-toward)
    mid = frames // 2
    crossing = jnp.logical_or(
        jnp.logical_and(f == mid - 1, core == 1), jnp.logical_and(f == mid, core == 0)
    )
    close = jnp.logical_and(near, jnp.logical_not(crossing))
    spare = jnp.logical_or(f < 2, f >= frames - 2)
    usual = jnp.logical_not(spare)
    spare_all = f < 2
    spare_half = jnp.logical_and(spare, f >= 2)
    whole = jnp.logical_or(spare_half, f // 2 == mid // 2)
    cut_some = jnp.logical_not(whole)
    by_way = jnp.logical_not(far_to)

    def in_use(group, there, upper):
        up = jnp.logical_and(upper == 1, group < BY_WAY_UP)
        down = jnp.logical_and(upper == 0, group < BY_WAY_DOWN)
        return jnp.logical_and(there, jnp.logical_or(up, down))

    def cross_by_way(group):
        return in_use(group, crossing, 1 - f // mid)

    def passes(group):
        return in_use(group, by_way, f // mid)

    def near_directly(group):
        return jnp.logical_and(near, jnp.logical_not(cross_by_way(group)))

    to_way = {"frame": f - toward * (mid - 1)}
    from_way = {"frame": f + toward * (mid - 2)}
    to_crossing = {"frame": f - toward * (mid - 2)}

    loads = [
        pltpu.make_async_copy(src, dst, in_sem.at[i])
        for i, (src, dst) in enumerate(
            (
                (tokens_hbm, tokens_ref),
                (ngain_hbm, ngain_ref),
                (qgain_hbm, qgain_ref),
                (kgain_hbm, kgain_ref),
                (lists_hbm, lists_ref),
                (counts_hbm, counts_ref),
                (wk_hbm, wk),
                (wv_hbm, wv),
                (wq_hbm, wq),
                (wo_hbm, wo.at[0:width]),
            )
        )
    ]
    loads[0].start()
    loads[1].start()

    barrier = pltpu.get_barrier_semaphore()

    def greet(device):
        pl.semaphore_signal(barrier, inc=1, device_id=device, device_id_type=MESH)

    for device in (to_right, to_left, to_other, to_sibling, to_across):
        greet(device)
    peers = 5
    for there, device in (
        (far_to, to_far),
        (far_from, {"frame": f - 2 * toward}),
        (near, to_near),
        (crossing, to_way),
        (crossing, from_way),
        (by_way, to_way),
        (by_way, to_crossing),
    ):
        pl.when(there)(functools.partial(greet, device))
        peers = peers + jnp.where(there, 1, 0)

    loads[0].wait()
    loads[1].wait()
    for copy in loads[2:]:
        copy.start()
    wide = tokens_ref[...].astype(jnp.float32)
    factor = lax.rsqrt(jnp.mean(wide * wide, axis=-1, keepdims=True) + EPS)
    xn[0] = (wide * factor * ngain_ref[...]).astype(jnp.bfloat16)

    pl.semaphore_wait(barrier, peers)

    sent = []

    def send(src, dst, sems, index, device, keep=True):
        copy = pltpu.make_async_remote_copy(
            src_ref=src,
            dst_ref=dst,
            send_sem=sems[0].at[index],
            recv_sem=sems[1].at[index],
            device_id=device,
            device_id_type=MESH,
        )
        if keep:
            sent.append(copy)
        return copy

    def rows_of(p):
        return pl.ds(p * piece, piece)

    ag = (ag_s, ag_r)
    a_right, a_left, b_other, f_ward, c_right, c_left, d_other = [], [], [], [], [], [], []
    c_full, e_other = [], []
    depth = xn.shape[2]
    cut = depth * 2 // 3
    most, rest, every = pl.ds(0, cut), pl.ds(cut, depth - cut), pl.ds(0, depth)
    for p in range(PIECES):
        r = rows_of(p)
        n = 8 * p
        a_right.append(send(xn.at[0, r], xn.at[3, r], ag, n, to_right))
        a_left.append(send(xn.at[0, r], xn.at[2, r], ag, n + 1, to_left))
        b_other.append(send(xn.at[0, r], xn.at[4, r], ag, n + 2, to_other))
        if p % 2:
            f_ward.append(send(xn.at[3, r], xn.at[1, r], ag, n + 3, to_right))
        else:
            f_ward.append(send(xn.at[2, r], xn.at[1, r], ag, n + 3, to_left))
        right_columns, left_columns = (most, every) if p % 2 else (every, most)
        c_right.append(
            send(xn.at[4, r, right_columns], xn.at[7, r, right_columns], ag, n + 4, to_right, False)
        )
        c_left.append(
            send(xn.at[4, r, left_columns], xn.at[6, r, left_columns], ag, n + 5, to_left, False)
        )
        if p % 2:
            c_full.append(send(xn.at[4, r], xn.at[7, r], ag, n + 4, to_right, False))
            e_other.append(send(xn.at[3, r, rest], xn.at[7, r, rest], ag, n + 7, to_other, False))
        else:
            c_full.append(send(xn.at[4, r], xn.at[6, r], ag, n + 5, to_left, False))
            e_other.append(send(xn.at[2, r, rest], xn.at[6, r, rest], ag, n + 7, to_other, False))
        d_other.append(send(xn.at[1, r], xn.at[5, r], ag, n + 6, to_other, False))
    g_right = send(xn.at[7, rows_of(2)], xn.at[5, rows_of(2)], ag, 22, to_right, False)
    g_left = send(xn.at[6, rows_of(3)], xn.at[5, rows_of(3)], ag, 30, to_left, False)
    g_first = send(xn.at[7, rows_of(0)], xn.at[5, rows_of(0)], ag, 6, to_right, False)
    g_second = send(xn.at[6, rows_of(1)], xn.at[5, rows_of(1)], ag, 14, to_left, False)

    def thrice(p, what):
        (getattr(c_left[p], what) if p % 2 else getattr(c_right[p], what))()
        cut_one = c_right[p] if p % 2 else c_left[p]

        @pl.when(cut_some)
        def _():
            getattr(cut_one, what)()
            if what != "start":
                getattr(e_other[p], what)()

        @pl.when(whole)
        def _():
            getattr(c_full[p], what)()

    def normed_heads(section, gain_ref):
        done = []
        for i in range(heads):
            part_i = section[:, i * HD : (i + 1) * HD]
            scale = lax.rsqrt(jnp.mean(part_i * part_i, axis=-1, keepdims=True) + EPS)
            done.append((part_i * scale * gain_ref[...]).astype(jnp.bfloat16))
        return done

    groups = (
        (0, 1, 0, rows),
        (2, 3, 0, rows),
        (1, 1, 0, rows),
        (5, 3, 0, half),
        (5, 3, half, piece),
        (5, 3, half + piece, piece),
    )

    def gathered(group):
        slot, count, low, each = groups[group]
        block = xn[slot : slot + count, low : low + each]
        return block.reshape(count * each, block.shape[-1])

    def kv_copy(group, kind):
        slot, count, low, each = groups[group]
        out, into, device, send_kind, recv_kind = (
            (BAND, BAND - toward, to_sibling, 0, 0),
            (BAND, BAND - 2 * toward, to_far, 1, 1),
            (BAND, BAND + toward, to_near, 2, 2),
            (BAND - toward, BAND - 2 * toward, to_sibling, 3, 3),
            (BAND, BAND - 2 * toward, to_way, 2, 3),
            (BAND + 2 * toward, BAND - toward, to_crossing, 1, 2),
        )[kind]
        r = pl.ds(low, each)
        return pltpu.make_async_remote_copy(
            src_ref=kv.at[pl.ds(out * 8 + slot, count), r],
            dst_ref=kv.at[pl.ds(into * 8 + slot, count), r],
            send_sem=kv_s.at[send_kind * len(groups) + group],
            recv_sem=kv_r.at[recv_kind * len(groups) + group],
            device_id=device,
            device_id_type=MESH,
        )

    def project_pairs(group):
        slot, count, low, each = groups[group]
        block = gathered(group)
        keys = jnp.dot(block, wk[...], preferred_element_type=jnp.float32)
        pieces = normed_heads(keys, kgain_ref)
        values = jnp.dot(block, wv[...], preferred_element_type=jnp.float32).astype(jnp.bfloat16)
        for n in range(count):
            at, r = BAND * 8 + slot + n, slice(n * each, (n + 1) * each)
            for i in range(heads):
                kv[at, low : low + each, i * HD : (i + 1) * HD] = pieces[i][r]
            kv[at, low : low + each, width:] = values[r]
        if group < BY_WAY:
            pl.when(near_directly(group))(lambda: kv_copy(group, 2).start())
            pl.when(cross_by_way(group))(lambda: kv_copy(group, 4).start())
        else:
            pl.when(near)(lambda: kv_copy(group, 2).start())
        pl.when(far_to)(lambda: kv_copy(group, 1).start())
        kv_copy(group, 0).start()

    def project_queries(group):
        slot, count, low, each = groups[group]
        queries = jnp.dot(gathered(group), wq[...], preferred_element_type=jnp.float32)
        pieces = normed_heads(queries, qgain_ref)
        for n in range(count):
            for i in range(heads):
                q[slot + n, low : low + each, i * HD : (i + 1) * HD] = pieces[i][
                    n * each : (n + 1) * each
                ]

    def pass_on(group):
        @pl.when(passes(group))
        def _():
            kv_copy(group, 3).wait_recv()
            kv_copy(group, 5).start()

    def relay(group, there):
        @pl.when(there)
        def _():
            kv_copy(group, 2).wait_recv()
            kv_copy(group, 3).start()

    for p in range(PIECES):
        a_right[(1, 3, 0, 2)[p]].start()
        a_left[p if p in (0, 3) else 3 - p].start()
        b_other[p].start()

    share = width // 2
    wo_send = send(
        wo_hbm.at[pl.ds(core * share, share)],
        wo.at[pl.ds(width + core * share, share)],
        (wo_s, wo_r),
        0,
        to_across,
    )
    wo_pass = send(
        wo.at[pl.ds(width + core * share, share)],
        wo.at[pl.ds(width + core * share, share)],
        (wo_s, wo_r),
        1,
        to_sibling,
    )
    wo_send.start()

    for copy in loads[2:8]:
        copy.wait()
    project_pairs(0)
    loads[8].wait()
    project_queries(0)

    for early, late in ((0, 1), (2, 3)):
        a_right[late].wait_recv()
        f_ward[late].start()
        pl.when(cut_some)(e_other[late].start)
        a_left[early].wait_recv()
        f_ward[early].start()
        pl.when(cut_some)(e_other[early].start)
    for p in range(PIECES):
        b_other[p].wait_recv()
        thrice(p, "start")
    for p in (0, 2):
        a_right[p].wait_recv()
        a_left[p + 1].wait_recv()
    project_pairs(1)
    for p in range(PIECES):
        f_ward[p].wait_recv()
        pl.when(f >= 2 if p < 2 else usual)(d_other[p].start)
    pass_on(0)
    project_queries(1)
    project_pairs(2)
    project_queries(2)
    relay(0, close)
    for first, last, group in ((0, 2, 3), (2, 3, 4), (3, 4, 5)):
        for p in range(first, last):
            if group == 3:
                thrice(p, "wait_recv")
        if group == 3:

            @pl.when(spare_all)
            def _():
                g_first.start()
                g_second.start()
                thrice(2, "wait_recv")
                g_right.start()
                thrice(3, "wait_recv")
                g_left.start()

        if group == 4:

            @pl.when(f >= 2)
            def _():
                thrice(2, "wait_recv")
                pl.when(spare_half)(g_right.start)
                thrice(3, "wait_recv")
                pl.when(spare_half)(g_left.start)

        for p in range(first, last):
            d_other[p].wait_recv()
        project_pairs(group)
        if group - 2 < BY_WAY:
            pass_on(group - 2)
        if group < 5:
            project_queries(group)
        relay(group - 2, close)
    project_queries(5)
    loads[9].wait()
    wo_send.wait_recv()
    wo_pass.start()
    relay(4, close)
    relay(5, close)
    for group in range(len(groups)):
        relay(group, crossing)

    for group in range(len(groups)):
        kv_copy(group, 0).wait_recv()

        @pl.when(far_from)
        def _():
            kv_copy(group, 1).wait_recv()

        @pl.when(far_to)
        def _():
            kv_copy(group, 3).wait_recv()

    score_factor = 1.0 / HD**0.5

    def attend(k):
        block = (x + k) % 4
        own = SLOT[k]
        queries = jnp.concatenate([q[own], q[own + 4]], axis=0)
        listed = counts_ref[block]
        pairs, on = [], []
        for m in range(MAXB):
            live = m < listed
            picked = jnp.where(live, lists_ref[block, m], f * NB + block)
            frame = jnp.clip(picked // NB - f + BAND, 0, 2 * BAND)
            across = (picked % NB - x + 4) % 4
            spot = frame * 8 + (across % 2) * 2 + across // 2
            pairs += [kv[spot], kv[spot + 4]]
            on.append(jnp.where(live, 1.0, 0.0).astype(jnp.float32))
        weighted, totals = [], []
        for i in range(heads):
            keys = jnp.concatenate([pair[:, i * HD : (i + 1) * HD] for pair in pairs], axis=0)
            values = jnp.concatenate(
                [pair[:, width + i * HD : width + (i + 1) * HD] for pair in pairs], axis=0
            )
            scores = lax.dot_general(
                queries[:, i * HD : (i + 1) * HD],
                keys,
                (((1,), (1,)), ((), ())),
                preferred_element_type=jnp.float32,
            )
            weights = [
                jnp.exp(scores[:, m * BLK : (m + 1) * BLK] * score_factor) * on[m]
                for m in range(MAXB)
            ]
            summed = functools.reduce(jnp.add, weights)
            totals.append(jnp.sum(summed, axis=-1, keepdims=True))
            rounded = jnp.concatenate([weight.astype(jnp.bfloat16) for weight in weights], axis=1)
            weighted.append(jnp.dot(rounded, values, preferred_element_type=jnp.float32))
        for i in range(heads):
            done = (weighted[i] / totals[i]).astype(jnp.bfloat16)
            ctx[k, 0, :, i * HD : (i + 1) * HD] = done[0:rows]
            ctx[k, 1, :, i * HD : (i + 1) * HD] = done[rows:]

    ctx_sends = [
        send(ctx.at[k, 1], ctx.at[k, 2], (ctx_s, ctx_r), k, to_other) for k in range(4)
    ]

    def out_project(k):
        partial = jnp.dot(ctx[k, 0], wo[0:width], preferred_element_type=jnp.float32)
        partial = partial + jnp.dot(ctx[k, 2], wo[width:], preferred_element_type=jnp.float32)
        part[k] = partial.astype(jnp.bfloat16)

    rs = (rs_s, rs_r)
    h_left, h_right, c_l, c_r = [], [], [], []
    for p in range(PIECES):
        r = rows_of(p)
        if p < PIECES // 2:
            h_left.append(send(part.at[2, r], got_h.at[r], rs, 3 * p, to_left))
        else:
            h_right.append(send(part.at[2, r], got_h.at[r], rs, 3 * p, to_right))
        c_l.append(send(part.at[3, r], from_right_hbm.at[r], rs, 3 * p + 1, to_left))
        c_r.append(send(part.at[1, r], from_left_hbm.at[r], rs, 3 * p + 2, to_right))

    for k in (2, 3, 1):
        attend(k)
        ctx_sends[k].start()
    wo_pass.wait_recv()
    ctx_sends[2].wait_recv()
    out_project(2)
    for p in range(2):
        h_left[p].start()
        h_right[p].start()
    attend(0)
    ctx_sends[0].start()
    ctx_sends[3].wait_recv()
    out_project(3)
    c_l[2].start()
    c_l[3].start()
    ctx_sends[1].wait_recv()
    out_project(1)
    c_r[0].start()
    c_r[1].start()

    def add_in(k, p):
        r = slice(p * piece, (p + 1) * piece)
        total = part[k, r].astype(jnp.float32) + got_h[r].astype(jnp.float32)
        part[k, r] = total.astype(jnp.bfloat16)

    for p in range(2):
        h_left[p].wait_recv()
        add_in(3, p)
        c_l[p].start()
        h_right[p].wait_recv()
        add_in(1, p + 2)
        c_r[p + 2].start()
    ctx_sends[0].wait_recv()
    out_project(0)
    mine = pltpu.make_async_copy(part.at[0], own_hbm, in_sem.at[0])
    mine.start()
    for p in (2, 3, 0, 1):
        c_l[p].wait_recv()
        c_r[(p + 2) % 4].wait_recv()
    mine.wait()

    for copy in sent + d_other:
        copy.wait_send()
    for p in range(PIECES):
        thrice(p, "wait_send")
    for group in range(len(groups)):
        kv_copy(group, 0).wait_send()
        ends = ((1, far_to), (2, near), (3, near))
        if group < BY_WAY:
            ends = ((1, far_to), (2, near_directly(group)), (3, near))
            ends += ((4, cross_by_way(group)), (5, passes(group)))
        for kind, there in ends:
            pl.when(there)(kv_copy(group, kind).wait_send)


def per_device(
    tokens,
    norm_gain,
    w_query,
    w_key,
    w_value,
    query_gain,
    key_gain,
    w_out,
    block_lists,
    block_counts,
):
    rows, depth = tokens.shape
    width = w_query.shape[1]
    dma = pltpu.SemaphoreType.DMA
    bf16 = jnp.bfloat16
    hbm = pl.BlockSpec(memory_space=pltpu.HBM)
    terms = pl.pallas_call(
        functools.partial(kernel, lax.axis_size("frame")),
        out_shape=[jax.ShapeDtypeStruct((rows, depth), bf16)] * 3,
        in_specs=[hbm] * 10,
        out_specs=[hbm] * 3,
        scratch_shapes=[
            pltpu.VMEM((rows, depth), bf16),
            pltpu.VMEM((1, depth), jnp.float32),
            pltpu.VMEM((1, HD), jnp.float32),
            pltpu.VMEM((1, HD), jnp.float32),
            pltpu.SMEM(block_lists.shape, jnp.int32),
            pltpu.SMEM(block_counts.shape, jnp.int32),
            pltpu.VMEM((depth, width), bf16),
            pltpu.VMEM((depth, width), bf16),
            pltpu.VMEM((depth, width), bf16),
            pltpu.VMEM((2 * width, depth), bf16),
            pltpu.VMEM((8, rows, depth), bf16),
            pltpu.VMEM((8, rows, width), bf16),
            pltpu.VMEM(((2 * BAND + 1) * 8, rows, 2 * width), bf16),
            pltpu.VMEM((4, 3, rows, width), bf16),
            pltpu.VMEM((4, rows, depth), bf16),
            pltpu.VMEM((rows, depth), bf16),
            dma((10,)),
            dma((8 * PIECES,)),
            dma((8 * PIECES,)),
            dma((24,)),
            dma((24,)),
            dma((2,)),
            dma((2,)),
            dma((4,)),
            dma((4,)),
            dma((3 * PIECES,)),
            dma((3 * PIECES,)),
        ],
        compiler_params=pltpu.CompilerParams(
            collective_id=0, has_side_effects=True, vmem_limit_bytes=63 * 1024 * 1024
        ),
    )(
        tokens,
        norm_gain.reshape(1, depth),
        query_gain.reshape(1, HD),
        key_gain.reshape(1, HD),
        block_lists,
        block_counts,
        w_query,
        w_key,
        w_value,
        w_out,
    )
    own, from_right, from_left = (term.astype(jnp.float32) for term in terms)
    return (own + from_right + from_left).astype(bf16)


def solution(mesh):
    placed = (
        P(("frame", "head"), None),
        P(),
        P(None, "head"),
        P(None, "head"),
        P(None, "head"),
        P(),
        P(),
        P("head", None),
        P("frame", None),
        P("frame"),
    )
    return jax.shard_map(
        per_device,
        mesh=mesh,
        in_specs=placed,
        out_specs=P(("frame", "head"), None),
        check_vma=False,
    )
```

```python
import functools

import jax
import jax.numpy as jnp
from jax import lax
from jax.experimental import pallas as pl
from jax.experimental.pallas import tpu as pltpu
from jax.sharding import PartitionSpec as P

HD = 128
BLK = 128
MAXB = 6
BAND = 2
NB = 4
EPS = 1e-06
PIECES = 4
BY_WAY_UP = 0
BY_WAY_DOWN = 2
BY_WAY = max(BY_WAY_UP, BY_WAY_DOWN)
MESH = pl.DeviceIdType.MESH

SLOT = (0, 2, 1, 3)


def kernel(
    frames,
    tokens_hbm,
    ngain_hbm,
    qgain_hbm,
    kgain_hbm,
    lists_hbm,
    counts_hbm,
    wq_hbm,
    wk_hbm,
    wv_hbm,
    wo_hbm,
    own_hbm,
    from_right_hbm,
    from_left_hbm,
    tokens_ref,
    ngain_ref,
    qgain_ref,
    kgain_ref,
    lists_ref,
    counts_ref,
    wq,
    wk,
    wv,
    wo,
    xn,
    q,
    kv,
    ctx,
    part,
    got_h,
    in_sem,
    ag_s,
    ag_r,
    kv_s,
    kv_r,
    wo_s,
    wo_r,
    ctx_s,
    ctx_r,
    rs_s,
    rs_r,
):
    f = lax.axis_index("frame")
    head = lax.axis_index("head")
    x, y = head // 2, head % 2
    core = f % 2
    toward = 1 - 2 * core
    right, left = (x + 1) % 4, (x + 3) % 4
    to_right, to_left = {"head": right * 2 + y}, {"head": left * 2 + y}
    to_other = {"head": x * 2 + 1 - y}
    to_sibling = {"frame": f + toward}
    to_far = {"frame": f + 2 * toward}
    to_near = {"frame": f - toward}
    to_across = {"frame": (f + frames // 2) % frames, "head": x * 2 + 1 - y}
    rows = tokens_ref.shape[0]
    half, piece = rows // 2, rows // PIECES
    width = wq.shape[1]
    heads = width // HD

    def within(d):
        return jnp.logical_and(f + d >= 0, f + d < frames)

    far_to, far_from, near = within(2 * toward), within(-2 * toward), within(-toward)
    mid = frames // 2
    crossing = jnp.logical_or(
        jnp.logical_and(f == mid - 1, core == 1), jnp.logical_and(f == mid, core == 0)
    )
    close = jnp.logical_and(near, jnp.logical_not(crossing))
    spare = jnp.logical_or(f < 2, f >= frames - 2)
    usual = jnp.logical_not(spare)
    spare_all = f < 2
    spare_half = jnp.logical_and(spare, f >= 2)
    whole = jnp.logical_or(spare_half, f // 2 == mid // 2)
    cut_some = jnp.logical_not(whole)
    by_way = jnp.logical_not(far_to)

    def in_use(group, there, upper):
        up = jnp.logical_and(upper == 1, group < BY_WAY_UP)
        down = jnp.logical_and(upper == 0, group < BY_WAY_DOWN)
        return jnp.logical_and(there, jnp.logical_or(up, down))

    def cross_by_way(group):
        return in_use(group, crossing, 1 - f // mid)

    def passes(group):
        return in_use(group, by_way, f // mid)

    def near_directly(group):
        return jnp.logical_and(near, jnp.logical_not(cross_by_way(group)))

    to_way = {"frame": f - toward * (mid - 1)}
    from_way = {"frame": f + toward * (mid - 2)}
    to_crossing = {"frame": f - toward * (mid - 2)}

    loads = [
        pltpu.make_async_copy(src, dst, in_sem.at[i])
        for i, (src, dst) in enumerate(
            (
                (tokens_hbm, tokens_ref),
                (ngain_hbm, ngain_ref),
                (qgain_hbm, qgain_ref),
                (kgain_hbm, kgain_ref),
                (lists_hbm, lists_ref),
                (counts_hbm, counts_ref),
                (wk_hbm, wk),
                (wv_hbm, wv),
                (wq_hbm, wq),
                (wo_hbm, wo.at[0:width]),
            )
        )
    ]
    loads[0].start()
    loads[1].start()

    barrier = pltpu.get_barrier_semaphore()

    def greet(device):
        pl.semaphore_signal(barrier, inc=1, device_id=device, device_id_type=MESH)

    for device in (to_right, to_left, to_other, to_sibling, to_across):
        greet(device)
    peers = 5
    for there, device in (
        (far_to, to_far),
        (far_from, {"frame": f - 2 * toward}),
        (near, to_near),
        (crossing, to_way),
        (crossing, from_way),
        (by_way, to_way),
        (by_way, to_crossing),
    ):
        pl.when(there)(functools.partial(greet, device))
        peers = peers + jnp.where(there, 1, 0)

    loads[0].wait()
    loads[1].wait()
    for copy in loads[2:]:
        copy.start()
    wide = tokens_ref[...].astype(jnp.float32)
    factor = lax.rsqrt(jnp.mean(wide * wide, axis=-1, keepdims=True) + EPS)
    xn[0] = (wide * factor * ngain_ref[...]).astype(jnp.bfloat16)

    pl.semaphore_wait(barrier, peers)

    sent = []

    def send(src, dst, sems, index, device, keep=True):
        copy = pltpu.make_async_remote_copy(
            src_ref=src,
            dst_ref=dst,
            send_sem=sems[0].at[index],
            recv_sem=sems[1].at[index],
            device_id=device,
            device_id_type=MESH,
        )
        if keep:
            sent.append(copy)
        return copy

    def rows_of(p):
        return pl.ds(p * piece, piece)

    ag = (ag_s, ag_r)
    a_right, a_left, b_other, f_ward, c_right, c_left, d_other = [], [], [], [], [], [], []
    c_full, e_other = [], []
    depth = xn.shape[2]
    cut = depth * 2 // 3
    most, rest, every = pl.ds(0, cut), pl.ds(cut, depth - cut), pl.ds(0, depth)
    for p in range(PIECES):
        r = rows_of(p)
        n = 8 * p
        a_right.append(send(xn.at[0, r], xn.at[3, r], ag, n, to_right))
        a_left.append(send(xn.at[0, r], xn.at[2, r], ag, n + 1, to_left))
        b_other.append(send(xn.at[0, r], xn.at[4, r], ag, n + 2, to_other))
        if p % 2:
            f_ward.append(send(xn.at[3, r], xn.at[1, r], ag, n + 3, to_right))
        else:
            f_ward.append(send(xn.at[2, r], xn.at[1, r], ag, n + 3, to_left))
        right_columns, left_columns = (most, every) if p % 2 else (every, most)
        c_right.append(
            send(xn.at[4, r, right_columns], xn.at[7, r, right_columns], ag, n + 4, to_right, False)
        )
        c_left.append(
            send(xn.at[4, r, left_columns], xn.at[6, r, left_columns], ag, n + 5, to_left, False)
        )
        if p % 2:
            c_full.append(send(xn.at[4, r], xn.at[7, r], ag, n + 4, to_right, False))
            e_other.append(send(xn.at[3, r, rest], xn.at[7, r, rest], ag, n + 7, to_other, False))
        else:
            c_full.append(send(xn.at[4, r], xn.at[6, r], ag, n + 5, to_left, False))
            e_other.append(send(xn.at[2, r, rest], xn.at[6, r, rest], ag, n + 7, to_other, False))
        d_other.append(send(xn.at[1, r], xn.at[5, r], ag, n + 6, to_other, False))
    g_right = send(xn.at[7, rows_of(2)], xn.at[5, rows_of(2)], ag, 22, to_right, False)
    g_left = send(xn.at[6, rows_of(3)], xn.at[5, rows_of(3)], ag, 30, to_left, False)
    g_first = send(xn.at[7, rows_of(0)], xn.at[5, rows_of(0)], ag, 6, to_right, False)
    g_second = send(xn.at[6, rows_of(1)], xn.at[5, rows_of(1)], ag, 14, to_left, False)

    def thrice(p, what):
        (getattr(c_left[p], what) if p % 2 else getattr(c_right[p], what))()
        cut_one = c_right[p] if p % 2 else c_left[p]

        @pl.when(cut_some)
        def _():
            getattr(cut_one, what)()
            if what != "start":
                getattr(e_other[p], what)()

        @pl.when(whole)
        def _():
            getattr(c_full[p], what)()

    def normed_heads(section, gain_ref):
        done = []
        for i in range(heads):
            part_i = section[:, i * HD : (i + 1) * HD]
            scale = lax.rsqrt(jnp.mean(part_i * part_i, axis=-1, keepdims=True) + EPS)
            done.append((part_i * scale * gain_ref[...]).astype(jnp.bfloat16))
        return done

    groups = (
        (0, 1, 0, rows),
        (2, 3, 0, rows),
        (1, 1, 0, rows),
        (5, 3, 0, half),
        (5, 3, half, piece),
        (5, 3, half + piece, piece),
    )

    def gathered(group):
        slot, count, low, each = groups[group]
        block = xn[slot : slot + count, low : low + each]
        return block.reshape(count * each, block.shape[-1])

    def kv_copy(group, kind):
        slot, count, low, each = groups[group]
        out, into, device, send_kind, recv_kind = (
            (BAND, BAND - toward, to_sibling, 0, 0),
            (BAND, BAND - 2 * toward, to_far, 1, 1),
            (BAND, BAND + toward, to_near, 2, 2),
            (BAND - toward, BAND - 2 * toward, to_sibling, 3, 3),
            (BAND, BAND - 2 * toward, to_way, 2, 3),
            (BAND + 2 * toward, BAND - toward, to_crossing, 1, 2),
        )[kind]
        r = pl.ds(low, each)
        return pltpu.make_async_remote_copy(
            src_ref=kv.at[pl.ds(out * 8 + slot, count), r],
            dst_ref=kv.at[pl.ds(into * 8 + slot, count), r],
            send_sem=kv_s.at[send_kind * len(groups) + group],
            recv_sem=kv_r.at[recv_kind * len(groups) + group],
            device_id=device,
            device_id_type=MESH,
        )

    def project_pairs(group):
        slot, count, low, each = groups[group]
        block = gathered(group)
        keys = jnp.dot(block, wk[...], preferred_element_type=jnp.float32)
        pieces = normed_heads(keys, kgain_ref)
        values = jnp.dot(block, wv[...], preferred_element_type=jnp.float32).astype(jnp.bfloat16)
        for n in range(count):
            at, r = BAND * 8 + slot + n, slice(n * each, (n + 1) * each)
            for i in range(heads):
                kv[at, low : low + each, i * HD : (i + 1) * HD] = pieces[i][r]
            kv[at, low : low + each, width:] = values[r]
        if group < BY_WAY:
            pl.when(near_directly(group))(lambda: kv_copy(group, 2).start())
            pl.when(cross_by_way(group))(lambda: kv_copy(group, 4).start())
        else:
            pl.when(near)(lambda: kv_copy(group, 2).start())
        pl.when(far_to)(lambda: kv_copy(group, 1).start())
        kv_copy(group, 0).start()

    def project_queries(group):
        slot, count, low, each = groups[group]
        queries = jnp.dot(gathered(group), wq[...], preferred_element_type=jnp.float32)
        pieces = normed_heads(queries, qgain_ref)
        for n in range(count):
            for i in range(heads):
                q[slot + n, low : low + each, i * HD : (i + 1) * HD] = pieces[i][
                    n * each : (n + 1) * each
                ]

    def pass_on(group):
        @pl.when(passes(group))
        def _():
            kv_copy(group, 3).wait_recv()
            kv_copy(group, 5).start()

    def relay(group, there):
        @pl.when(there)
        def _():
            kv_copy(group, 2).wait_recv()
            kv_copy(group, 3).start()

    for p in range(PIECES):
        a_right[(1, 3, 0, 2)[p]].start()
        a_left[p if p in (0, 3) else 3 - p].start()
        b_other[p].start()

    share = width // 2
    wo_send = send(
        wo_hbm.at[pl.ds(core * share, share)],
        wo.at[pl.ds(width + core * share, share)],
        (wo_s, wo_r),
        0,
        to_across,
    )
    wo_pass = send(
        wo.at[pl.ds(width + core * share, share)],
        wo.at[pl.ds(width + core * share, share)],
        (wo_s, wo_r),
        1,
        to_sibling,
    )
    wo_send.start()

    for copy in loads[2:8]:
        copy.wait()
    project_pairs(0)
    loads[8].wait()
    project_queries(0)

    for early, late in ((0, 1), (2, 3)):
        a_right[late].wait_recv()
        f_ward[late].start()
        pl.when(cut_some)(e_other[late].start)
        a_left[early].wait_recv()
        f_ward[early].start()
        pl.when(cut_some)(e_other[early].start)
    for p in range(PIECES):
        b_other[p].wait_recv()
        thrice(p, "start")
    for p in (0, 2):
        a_right[p].wait_recv()
        a_left[p + 1].wait_recv()
    project_pairs(1)
    for p in range(PIECES):
        f_ward[p].wait_recv()
        pl.when(f >= 2 if p < 2 else usual)(d_other[p].start)
    pass_on(0)
    project_queries(1)
    project_pairs(2)
    project_queries(2)
    relay(0, close)
    for first, last, group in ((0, 2, 3), (2, 3, 4), (3, 4, 5)):
        for p in range(first, last):
            if group == 3:
                thrice(p, "wait_recv")
        if group == 3:

            @pl.when(spare_all)
            def _():
                g_first.start()
                g_second.start()
                thrice(2, "wait_recv")
                g_right.start()
                thrice(3, "wait_recv")
                g_left.start()

        if group == 4:

            @pl.when(f >= 2)
            def _():
                thrice(2, "wait_recv")
                pl.when(spare_half)(g_right.start)
                thrice(3, "wait_recv")
                pl.when(spare_half)(g_left.start)

        for p in range(first, last):
            d_other[p].wait_recv()
        project_pairs(group)
        if group - 2 < BY_WAY:
            pass_on(group - 2)
        if group < 5:
            project_queries(group)
        relay(group - 2, close)
    project_queries(5)
    loads[9].wait()
    wo_send.wait_recv()
    wo_pass.start()
    relay(4, close)
    relay(5, close)
    for group in range(len(groups)):
        relay(group, crossing)

    for group in range(len(groups)):
        kv_copy(group, 0).wait_recv()

        @pl.when(far_from)
        def _():
            kv_copy(group, 1).wait_recv()

        @pl.when(far_to)
        def _():
            kv_copy(group, 3).wait_recv()

    score_factor = 1.0 / HD**0.5

    def attend(k):
        block = (x + k) % 4
        own = SLOT[k]
        queries = jnp.concatenate([q[own], q[own + 4]], axis=0)
        listed = counts_ref[block]
        pairs, on = [], []
        for m in range(MAXB):
            live = m < listed
            picked = jnp.where(live, lists_ref[block, m], f * NB + block)
            frame = jnp.clip(picked // NB - f + BAND, 0, 2 * BAND)
            across = (picked % NB - x + 4) % 4
            spot = frame * 8 + (across % 2) * 2 + across // 2
            pairs += [kv[spot], kv[spot + 4]]
            on.append(jnp.where(live, 1.0, 0.0).astype(jnp.float32))
        weighted, totals = [], []
        for i in range(heads):
            keys = jnp.concatenate([pair[:, i * HD : (i + 1) * HD] for pair in pairs], axis=0)
            values = jnp.concatenate(
                [pair[:, width + i * HD : width + (i + 1) * HD] for pair in pairs], axis=0
            )
            scores = lax.dot_general(
                queries[:, i * HD : (i + 1) * HD],
                keys,
                (((1,), (1,)), ((), ())),
                preferred_element_type=jnp.float32,
            )
            weights = [
                jnp.exp(scores[:, m * BLK : (m + 1) * BLK] * score_factor) * on[m]
                for m in range(MAXB)
            ]
            summed = functools.reduce(jnp.add, weights)
            totals.append(jnp.sum(summed, axis=-1, keepdims=True))
            rounded = jnp.concatenate([weight.astype(jnp.bfloat16) for weight in weights], axis=1)
            weighted.append(jnp.dot(rounded, values, preferred_element_type=jnp.float32))
        for i in range(heads):
            done = (weighted[i] / totals[i]).astype(jnp.bfloat16)
            ctx[k, 0, :, i * HD : (i + 1) * HD] = done[0:rows]
            ctx[k, 1, :, i * HD : (i + 1) * HD] = done[rows:]

    ctx_sends = [
        send(ctx.at[k, 1], ctx.at[k, 2], (ctx_s, ctx_r), k, to_other) for k in range(4)
    ]

    def out_project(k):
        partial = jnp.dot(ctx[k, 0], wo[0:width], preferred_element_type=jnp.float32)
        ctx_sends[k].wait_recv()
        if k == 2:
            wo_pass.wait_recv()
        partial = partial + jnp.dot(ctx[k, 2], wo[width:], preferred_element_type=jnp.float32)
        part[k] = partial.astype(jnp.bfloat16)

    rs = (rs_s, rs_r)
    h_left, h_right, c_l, c_r = [], [], [], []
    for p in range(PIECES):
        r = rows_of(p)
        if p < PIECES // 2:
            h_left.append(send(part.at[2, r], got_h.at[r], rs, 3 * p, to_left))
        else:
            h_right.append(send(part.at[2, r], got_h.at[r], rs, 3 * p, to_right))
        c_l.append(send(part.at[3, r], from_right_hbm.at[r], rs, 3 * p + 1, to_left))
        c_r.append(send(part.at[1, r], from_left_hbm.at[r], rs, 3 * p + 2, to_right))

    for k in (2, 3, 1):
        attend(k)
        ctx_sends[k].start()
    out_project(2)
    for p in range(2):
        h_left[p].start()
        h_right[p].start()
    attend(0)
    ctx_sends[0].start()
    out_project(3)
    c_l[2].start()
    c_l[3].start()
    out_project(1)
    c_r[0].start()
    c_r[1].start()

    def add_in(k, p):
        r = slice(p * piece, (p + 1) * piece)
        total = part[k, r].astype(jnp.float32) + got_h[r].astype(jnp.float32)
        part[k, r] = total.astype(jnp.bfloat16)

    for p in range(2):
        h_left[p].wait_recv()
        add_in(3, p)
        c_l[p].start()
        h_right[p].wait_recv()
        add_in(1, p + 2)
        c_r[p + 2].start()
    out_project(0)
    mine = pltpu.make_async_copy(part.at[0], own_hbm, in_sem.at[0])
    mine.start()
    for p in (2, 3, 0, 1):
        c_l[p].wait_recv()
        c_r[(p + 2) % 4].wait_recv()
    mine.wait()

    for copy in sent + d_other:
        copy.wait_send()
    for p in range(PIECES):
        thrice(p, "wait_send")
    for group in range(len(groups)):
        kv_copy(group, 0).wait_send()
        ends = ((1, far_to), (2, near), (3, near))
        if group < BY_WAY:
            ends = ((1, far_to), (2, near_directly(group)), (3, near))
            ends += ((4, cross_by_way(group)), (5, passes(group)))
        for kind, there in ends:
            pl.when(there)(kv_copy(group, kind).wait_send)


def per_device(
    tokens,
    norm_gain,
    w_query,
    w_key,
    w_value,
    query_gain,
    key_gain,
    w_out,
    block_lists,
    block_counts,
):
    rows, depth = tokens.shape
    width = w_query.shape[1]
    dma = pltpu.SemaphoreType.DMA
    bf16 = jnp.bfloat16
    hbm = pl.BlockSpec(memory_space=pltpu.HBM)
    terms = pl.pallas_call(
        functools.partial(kernel, lax.axis_size("frame")),
        out_shape=[jax.ShapeDtypeStruct((rows, depth), bf16)] * 3,
        in_specs=[hbm] * 10,
        out_specs=[hbm] * 3,
        scratch_shapes=[
            pltpu.VMEM((rows, depth), bf16),
            pltpu.VMEM((1, depth), jnp.float32),
            pltpu.VMEM((1, HD), jnp.float32),
            pltpu.VMEM((1, HD), jnp.float32),
            pltpu.SMEM(block_lists.shape, jnp.int32),
            pltpu.SMEM(block_counts.shape, jnp.int32),
            pltpu.VMEM((depth, width), bf16),
            pltpu.VMEM((depth, width), bf16),
            pltpu.VMEM((depth, width), bf16),
            pltpu.VMEM((2 * width, depth), bf16),
            pltpu.VMEM((8, rows, depth), bf16),
            pltpu.VMEM((8, rows, width), bf16),
            pltpu.VMEM(((2 * BAND + 1) * 8, rows, 2 * width), bf16),
            pltpu.VMEM((4, 3, rows, width), bf16),
            pltpu.VMEM((4, rows, depth), bf16),
            pltpu.VMEM((rows, depth), bf16),
            dma((10,)),
            dma((8 * PIECES,)),
            dma((8 * PIECES,)),
            dma((24,)),
            dma((24,)),
            dma((2,)),
            dma((2,)),
            dma((4,)),
            dma((4,)),
            dma((3 * PIECES,)),
            dma((3 * PIECES,)),
        ],
        compiler_params=pltpu.CompilerParams(
            collective_id=0, has_side_effects=True, vmem_limit_bytes=63 * 1024 * 1024
        ),
    )(
        tokens,
        norm_gain.reshape(1, depth),
        query_gain.reshape(1, HD),
        key_gain.reshape(1, HD),
        block_lists,
        block_counts,
        w_query,
        w_key,
        w_value,
        w_out,
    )
    own, from_right, from_left = (term.astype(jnp.float32) for term in terms)
    return (own + from_right + from_left).astype(bf16)


def solution(mesh):
    placed = (
        P(("frame", "head"), None),
        P(),
        P(None, "head"),
        P(None, "head"),
        P(None, "head"),
        P(),
        P(),
        P("head", None),
        P("frame", None),
        P("frame"),
    )
    return jax.shard_map(
        per_device,
        mesh=mesh,
        in_specs=placed,
        out_specs=P(("frame", "head"), None),
        check_vma=False,
    )
```
